32 devices in a mesh: prow: 2 (over x), pcol: 4 (over z), dz: 4 (over y, core).
Axes of the slice: x: 2, y: 2, z: 4, core: 2. Of those that a mesh axis runs over, the one named last changes fastest.
Arguments:
- coeffs: bfloat16 [1024, 512], P('prow', 'pcol'), may hold values from -0.25 to 0.25
- occupations: int32 [512], P('pcol'), may hold values from 0 to 2
- counts: int32 [64], replicated, may hold values from 5 to 13
- intersection: int32 [32, 8], replicated, may hold values from 0 to 63, as said below
- phi_values: bfloat16 [4096, 128], P(('prow', 'pcol', 'dz')), may hold values from -0.5 to 0.5
- panel_values: bfloat16 [4096, 512], P(('prow', 'pcol', 'dz')), may hold values from -6 to 6
- proj_site: bfloat16 [64, 16, 16], P(('prow', 'pcol')), may hold values from -1.5 to 1.5
- proj_panel: bfloat16 [64, 16, 512], P(('prow', 'pcol'), None, 'dz'), may hold values from -6 to 6
Outputs:
- density: float32 [4096], P(('prow', 'pcol', 'dz'))
- rho_ij: float32 [64, 256], P(('prow', 'pcol'))
The draws below stay inside these ranges and needn't reach their ends.
Inputs may be any that keep to these rules, and one draw needn't show every extreme that they name: `intersection`: each domain lists 8 distinct atoms in no particular order; of the 8 atoms a * 8 .. (a + 1) * 8 - 1 of any owner a, a domain lists either none or exactly 2, and exactly 4 owners have 2 each.
All inputs are finite; a program needn't handle non-finite values.
Results may differ from the reference program's by a relative error of at most 0.0029.
Values may be sent and summed in bfloat16 or wider, within the bound.
No kernel may reach another device: no remote copies, remote signals or barrier semaphores. Data moves between devices by JAX's collectives and lax.ppermute only.
A program may use at most 64 MiB of HBM per device.

```python
import jax
import jax.numpy as jnp
from jax import lax

SLOTS = 16
NPROJ = 16
PW = 512
NA_OWN = 8
CAP = 2
CELLS_DEV = 128
NA = 64
NB = 1024
NST = 512
OWNERS_DOM = 4
OV = 8
DOMAINS = 32


def draw_intersection(key, part):
    key = jax.random.fold_in(key, 7)
    owners_all = NA // NA_OWN

    def one_domain(dkey):
        first, second, third = jax.random.split(dkey, 3)
        owners = jax.random.permutation(first, owners_all)[:OWNERS_DOM]
        locals_ = jax.vmap(lambda kk: jax.random.permutation(kk, NA_OWN)[:CAP])(jax.random.split(second, OWNERS_DOM))
        atoms = (owners[:, None] * NA_OWN + locals_).reshape(-1)
        order = jax.random.permutation(third, OV)
        return atoms[order].astype(jnp.int32)
    return jax.vmap(one_domain)(jax.random.split(key, DOMAINS))


def place_ends(array, key, low, top_value):
    longest = array.shape.index(max(array.shape))
    spots = []
    for shift in (0, 1):
        where = [jax.random.randint(jax.random.fold_in(key, axis), (), 0, length) for axis, length in enumerate(array.shape)]
        where[longest] = (where[longest] + shift) % array.shape[longest]
        spots.append(tuple(where))
    return array.at[spots[0]].set(low).at[spots[1]].set(top_value)


def levels(stream_key, extent, shards, least, largest):
    def one(dim, shards_of):
        steps = jax.random.uniform(jax.random.fold_in(jax.random.fold_in(stream_key, 6), dim), (shards_of,), jnp.float32, least / len(shards), largest / len(shards))
        return jnp.repeat(jnp.exp(steps), extent[dim] // shards_of).reshape((-1,) + (1,) * (len(extent) - dim - 1))

    loudness = one(*shards[0])
    for cut in shards[1:]:
        loudness = loudness * one(*cut)
    return loudness


def noise(key, extent, spread, limit, cuts=(), kind=jnp.bfloat16):
    drawn = spread * jax.random.normal(key, extent, jnp.float32)
    if cuts:
        drawn = drawn * levels(key, extent, cuts, -0.22, 0.18)
    return jnp.clip(drawn, -limit, limit).astype(kind)


def setup_inputs(seed: int = 0) -> dict:
    key_list = jax.random.split(jax.random.key(seed), 9)
    return {
        "coeffs": noise(key_list[0], (NB, NST), NST ** -0.5, 0.25, ((0, 2), (1, 4))),
        "occupations": place_ends(jax.random.randint(key_list[1], (NST,), 0, 3), jax.random.fold_in(key_list[1], 1), 0, 2).astype(jnp.int32),
        "counts": place_ends(jax.random.randint(key_list[2], (NA,), 5, 14), jax.random.fold_in(key_list[2], 1), 5, 13).astype(jnp.int32),
        "intersection": draw_intersection(jax.random.fold_in(key_list[8], 71), 0),
        "phi_values": noise(key_list[4], (DOMAINS * CELLS_DEV, OV * SLOTS), (OV * SLOTS) ** -0.5, 0.5, ((0, 32),)),
        "panel_values": noise(key_list[5], (DOMAINS * CELLS_DEV, PW), 1.0, 6.0, ((0, 32),)),
        "proj_site": noise(key_list[6], (NA, NPROJ, SLOTS), SLOTS ** -0.5, 1.5, ((0, 8),)),
        "proj_panel": noise(key_list[7], (NA, NPROJ, PW), 1.0, 6.0, ((0, 8), (2, 4))),
    }


def reference(coeffs, occupations, counts, intersection, phi_values, panel_values, proj_site, proj_panel):
    slot_ids = jnp.arange(SLOTS, dtype=jnp.int32)
    live = (slot_ids[None, :] < counts[:, None]).reshape(NB, 1)
    masked = jnp.where(live, coeffs, jnp.zeros((), coeffs.dtype))
    weights = (occupations.astype(jnp.float32) * 0.5).astype(coeffs.dtype)
    scaled = masked * weights[None, :]
    panel_p = lax.dot_general(scaled, masked[:PW], (((1,), (1,)), ((), ())), preferred_element_type=jnp.float32).astype(jnp.bfloat16)
    blocks = panel_p.reshape(NA, SLOTS, PW)
    phi_three = phi_values.reshape(DOMAINS, CELLS_DEV, OV * SLOTS)
    pan_three = panel_values.reshape(DOMAINS, CELLS_DEV, PW)

    def one_domain(items):
        listed, phi_dom, pan_dom = items
        rows_dom = blocks[listed].reshape(OV * SLOTS, PW)
        mixed = jnp.dot(phi_dom, rows_dom, preferred_element_type=jnp.float32)
        return jnp.sum(mixed * pan_dom.astype(jnp.float32), axis=1)

    density = lax.map(one_domain, (intersection, phi_three, pan_three)).reshape(-1)
    projected = jnp.einsum("aim,amn->ain", proj_site, blocks, preferred_element_type=jnp.float32)
    rho_full = jnp.einsum("ain,ajn->aij", projected, proj_panel.astype(jnp.float32), precision=lax.Precision.HIGHEST)
    return density, rho_full.reshape(NA, NPROJ * NPROJ)
```

```python
import functools

import jax
import jax.numpy as jnp
from jax import lax
from jax.experimental import pallas as pl
from jax.experimental.pallas import tpu as pltpu
from jax.sharding import PartitionSpec as P

SLOTS = 16
LIVE = 13
NPROJ = 16
PW = 512
CAP = 2
GATHER_LIMIT = 2**21

F32 = jnp.float32
BF16 = jnp.bfloat16


def spread(block, axis, holder):
    block = jnp.where(lax.axis_index(axis) == holder, block, jnp.zeros_like(block))
    return lax.psum(block, axis)


def exchange_shards(
    coeffs, occupations, counts, intersection, phi_values, panel_values, proj_site, proj_panel
):
    n_row = lax.axis_size("prow")
    n_col = lax.axis_size("pcol")
    n_slab = lax.axis_size("dz")
    rows_blk = coeffs.shape[0]
    atoms_blk = rows_blk // SLOTS
    start_atom = lax.axis_index("prow") * atoms_blk
    block_counts = lax.dynamic_slice_in_dim(counts, start_atom, atoms_blk)
    slot_ids = lax.broadcasted_iota(jnp.int32, (atoms_blk, SLOTS), 1)
    live = (slot_ids < block_counts[:, None]).reshape(rows_blk, 1)
    masked = jnp.where(live, coeffs, jnp.zeros((), coeffs.dtype))
    weights = (occupations.astype(jnp.float32) * 0.5).astype(coeffs.dtype)
    panel = spread(coeffs[:PW], "prow", 0)
    panel_slots = lax.broadcasted_iota(jnp.int32, (PW // SLOTS, SLOTS), 1)
    panel_live = (panel_slots < counts[: PW // SLOTS][:, None]).reshape(PW, 1)
    panel = jnp.where(panel_live, panel, jnp.zeros((), panel.dtype))
    scaled = masked * weights[None, :]
    owned = lax.psum_scatter(
        lax.dot_general(
            scaled, panel, (((1,), (1,)), ((), ())), preferred_element_type=jnp.float32
        ),
        "pcol",
        scatter_dimension=0,
        tiled=True,
    )
    owned_rows = owned.astype(jnp.bfloat16)
    atoms_own = owned_rows.shape[0] // SLOTS
    owned_blocks = owned_rows.reshape(atoms_own, SLOTS, PW)
    owner_id = lax.axis_index("prow") * n_col + lax.axis_index("pcol")
    slab = lax.axis_index("dz")
    receivers = n_row * n_col
    by_slab = intersection.reshape(receivers, n_slab, intersection.shape[1])
    lists = lax.dynamic_index_in_dim(by_slab, slab, 1, keepdims=False)
    mine = lists // atoms_own == owner_id
    ranks = jnp.cumsum(mine.astype(jnp.int32), axis=1) - 1
    slot_pick = lax.broadcasted_iota(jnp.int32, (1, 1, CAP), 2)
    picked = mine[:, :, None] & (ranks[:, :, None] == slot_pick)
    local_atom = jnp.sum(jnp.where(picked, (lists - owner_id * atoms_own)[:, :, None], 0), axis=1)
    valid = jnp.any(picked, axis=1)
    outgoing = jnp.where(
        valid[:, :, None, None], owned_blocks[local_atom], jnp.zeros((), owned_rows.dtype)
    )
    incoming = lax.all_to_all(
        outgoing.reshape(receivers * CAP * SLOTS, PW),
        ("prow", "pcol"),
        split_axis=0,
        concat_axis=0,
        tiled=True,
    )
    incoming = incoming.reshape(receivers * CAP, SLOTS, PW)
    domain = owner_id * n_slab + slab
    wanted = lax.dynamic_index_in_dim(intersection, domain, 0, keepdims=False)
    wanted_owner = wanted // atoms_own
    listed = wanted.shape[0]
    same_owner = wanted_owner[:, None] == wanted_owner[None, :]
    earlier = lax.broadcasted_iota(jnp.int32, (listed, listed), 1) < lax.broadcasted_iota(
        jnp.int32, (listed, listed), 0
    )
    rank_in = jnp.sum((same_owner & earlier).astype(jnp.int32), axis=1)
    slot_of = wanted_owner * CAP + rank_in
    domain_rows = incoming[slot_of].reshape(listed * SLOTS, PW)
    mixed = jnp.dot(phi_values, domain_rows, preferred_element_type=jnp.float32)
    density = jnp.sum(mixed * panel_values.astype(jnp.float32), axis=1)
    projected = jnp.einsum(
        "aim,amn->ain", proj_site, owned_blocks, preferred_element_type=jnp.float32
    )
    slab_cols = proj_panel.shape[2]
    part_proj = lax.dynamic_slice_in_dim(projected, slab * slab_cols, slab_cols, 2)
    partial_rho = jnp.einsum(
        "ain,ajn->aij", part_proj, proj_panel.astype(jnp.float32), precision=lax.Precision.HIGHEST
    )
    rho_full = lax.psum(partial_rho, "dz")
    return (density, rho_full.reshape(atoms_own, NPROJ * NPROJ))


def iota(shape, dim):
    return lax.broadcasted_iota(jnp.int32, shape, dim)


def pick(condition):
    return jnp.where(condition, 1.0, 0.0).astype(BF16)


def take(left, right):
    return jnp.dot(left, right, preferred_element_type=F32).astype(BF16)


def packed_rows(rows):
    return rows // SLOTS * LIVE + 16


def pack_kernel(counts_ref, occ_ref, coeffs_ref, out_ref):
    rows = coeffs_ref.shape[0]
    atoms = rows // SLOTS
    first = lax.axis_index("prow") * atoms
    group = 16
    old = iota((group * LIVE, group * SLOTS), 1)
    new = iota((group * LIVE, group * SLOTS), 0)
    slot = old & (SLOTS - 1)
    move = pick(((old >> 4) * LIVE + slot == new) & (slot < LIVE))
    lane_slot = iota((SLOTS, coeffs_ref.shape[1]), 0)
    for g in range(atoms // group):
        tiles = []
        for a in range(group):
            at = (g * group + a) * SLOTS
            tile = coeffs_ref[at : at + SLOTS, :]
            tiles.append(jnp.where(lane_slot < counts_ref[first + g * group + a], tile, jnp.zeros_like(tile)))
        block = jnp.concatenate(tiles, axis=0)
        out_ref[g * group * LIVE : (g + 1) * group * LIVE, :] = jnp.dot(
            move, block, preferred_element_type=F32
        ).astype(BF16)
    weights = occ_ref[...].astype(F32) * 0.5
    out_ref[atoms * LIVE :, :] = jnp.broadcast_to(weights, (16, weights.shape[1])).astype(BF16)


def left_kernel(n_col, n_slab, lists_ref, phi_ref, panel_ref, site_ref, proj_ref, out_ref):
    x, z, s = lax.axis_index("prow"), lax.axis_index("pcol"), lax.axis_index("dz")
    cells, listed = phi_ref.shape[0], lists_ref.shape[1]
    packed = out_ref.shape[2]
    own = site_ref.shape[0]
    atoms_own = own // NPROJ
    blk_atoms = (packed - 16) // LIVE
    domain = (x * n_col + z) * n_slab + s
    slot = iota((SLOTS, packed), 0)
    new = iota((SLOTS, packed), 1)
    old = iota((PW, packed), 0)
    to_panel = pick(
        ((old >> 4) * LIVE + (old & (SLOTS - 1)) == iota((PW, packed), 1)) & ((old & (SLOTS - 1)) < LIVE)
    )
    panel_side = take(jnp.concatenate([panel_ref[...], proj_ref[...]], axis=0), to_panel)
    spread_lanes = pick(iota((SLOTS, own), 0) == (iota((SLOTS, own), 1) & (SLOTS - 1)))
    tiled = take(site_ref[...], spread_lanes)
    mine = (iota((own, own), 0) & (atoms_own - 1)) == (iota((own, own), 1) >> 4)
    tiled = jnp.where(mine, tiled, jnp.zeros_like(tiled))
    to_own = jnp.concatenate(
        [pick((new == (z * atoms_own + a) * LIVE + slot) & (slot < LIVE)) for a in range(atoms_own)], axis=0
    )
    site_side = take(tiled, to_own)
    for b in range(2):
        to_listed = jnp.concatenate(
            [
                pick(
                    (new == (lists_ref[domain, p] - b * blk_atoms) * LIVE + slot)
                    & (slot < LIVE)
                    & (new < blk_atoms * LIVE)
                )
                for p in range(listed)
            ],
            axis=0,
        )
        out_ref[b, 0:cells, :] = take(phi_ref[...], to_listed)
        if b == 0:
            out_ref[b, cells : 2 * cells, :] = panel_side[:cells]
            out_ref[b, 2 * cells + own :, :] = panel_side[cells:]
        else:
            out_ref[b, cells : 2 * cells, :] = jnp.zeros((cells, packed), BF16)
            out_ref[b, 2 * cells + own :, :] = jnp.zeros((own, packed), BF16)
        out_ref[b, 2 * cells : 2 * cells + own, :] = jnp.where(x == b, site_side, jnp.zeros_like(site_side))


def sum_kernel(n_pairs, cells, left_ref, *refs):
    blocks, (density_ref, rho_ref) = refs[: 2 * n_pairs], refs[2 * n_pairs :]
    x = lax.axis_index("prow")
    swapped = x ^ (lax.axis_index("dz") & 1)
    own = left_ref.shape[1] - 2 * cells
    own = own // 2
    weight_row = left_ref.shape[2] - 16
    total = None
    rho = None
    for k in range(n_pairs):
        near = x if k == 0 else swapped
        a_ref, b_ref = blocks[2 * k], blocks[2 * k + 1]
        r = jnp.dot(left_ref[near], a_ref[...], preferred_element_type=F32)
        r += jnp.dot(left_ref[1 - near], b_ref[...], preferred_element_type=F32)
        f = a_ref[weight_row : weight_row + 16, :].astype(F32)[0:1]
        term = r[:cells] * f * r[cells : 2 * cells]
        part = lax.dot_general(
            r[2 * cells : 2 * cells + own] * f,
            r[2 * cells + own :],
            (((1,), (1,)), ((), ())),
            precision=lax.Precision.HIGHEST,
            preferred_element_type=F32,
        )
        total = term if total is None else total + term
        rho = part if rho is None else rho + part
    density_ref[...] = jnp.sum(total.T, axis=0, keepdims=True)
    atoms = own // NPROJ
    rho = jnp.where((iota((own, own), 0) & (atoms - 1)) == (iota((own, own), 1) >> 4), rho, 0.0)
    wide = NPROJ * NPROJ
    fold = jnp.where(
        (iota((own, wide), 0) & (NPROJ - 1)) == (iota((own, wide), 1) & (NPROJ - 1)), 1.0, 0.0
    ).astype(F32)
    rows = jnp.dot(rho, fold, precision=lax.Precision.HIGHEST, preferred_element_type=F32)
    keep = (iota((own, wide), 0) // atoms) == (iota((own, wide), 1) >> 4)
    rho_ref[...] = jnp.sum(jnp.where(keep, rows, 0.0).reshape(NPROJ, atoms, wide), axis=0)


VMEM = pl.BlockSpec(memory_space=pltpu.VMEM)
SMEM = pl.BlockSpec(memory_space=pltpu.SMEM)
PARAMS = pltpu.CompilerParams(vmem_limit_bytes=32 * 2**20)


def gather_shards(
    coeffs, occupations, counts, intersection, phi_values, panel_values, proj_site, proj_panel
):
    n_row, n_col, n_slab = (lax.axis_size(a) for a in ("prow", "pcol", "dz"))
    axes = ("prow", "pcol", "dz")

    def move(block, target):
        pairs = []
        for i in range(n_row * n_col * n_slab):
            x, z, s = i // (n_col * n_slab), i // n_slab % n_col, i % n_slab
            tx, tz, ts = target(x, z, s)
            pairs.append((i, (tx * n_col + tz) * n_slab + ts))
        return lax.ppermute(block, axes, pairs)

    rows, states = coeffs.shape
    packed = packed_rows(rows)
    atoms_own = proj_site.shape[0]
    own = atoms_own * NPROJ
    cells = phi_values.shape[0]
    block = pl.pallas_call(
        pack_kernel,
        out_shape=jax.ShapeDtypeStruct((packed, states), BF16),
        in_specs=[SMEM, VMEM, VMEM],
        out_specs=VMEM,
        compiler_params=PARAMS,
    )(counts, occupations.reshape(1, states), coeffs)
    got = {}
    for k in list(range(n_col - 1, 0, -1)):
        got[k] = move(block, lambda x, z, s: (x ^ (s & 1), z ^ k, s))
    other = move(block, lambda x, z, s: (x ^ 1, z, s))
    half = move(proj_panel, lambda x, z, s: (x, z, s ^ 2))
    slab = lax.axis_index("dz")
    mine_first = (slab & 2) == 0
    pair = jnp.stack([jnp.where(mine_first, proj_panel, half), jnp.where(mine_first, half, proj_panel)])
    swap = move(pair, lambda x, z, s: (x, z, s ^ 1))
    even = (slab & 1) == 0
    evens, odds = jnp.where(even, pair, swap), jnp.where(even, swap, pair)
    whole = jnp.stack([evens[0], odds[0], evens[1], odds[1]], axis=2).reshape(own, PW)
    site = proj_site.transpose(1, 0, 2).reshape(own, SLOTS)
    left = pl.pallas_call(
        functools.partial(left_kernel, n_col, n_slab),
        out_shape=jax.ShapeDtypeStruct((2, 2 * cells + 2 * own, packed), BF16),
        in_specs=[SMEM, VMEM, VMEM, VMEM, VMEM],
        out_specs=VMEM,
        compiler_params=PARAMS,
        cost_estimate=pl.CostEstimate(flops=2 * 10**8, bytes_accessed=2 * 10**6, transcendentals=0),
    )(intersection, phi_values, panel_values, site, whole)
    blocks = [block, other]
    for k in got:
        blocks += [got[k], move(got[k], lambda x, z, s: (x, z, s ^ 1))]
    density, rho = pl.pallas_call(
        functools.partial(sum_kernel, n_col, cells),
        out_shape=(
            jax.ShapeDtypeStruct((1, cells), F32),
            jax.ShapeDtypeStruct((atoms_own, NPROJ * NPROJ), F32),
        ),
        in_specs=[VMEM] * (1 + len(blocks)),
        out_specs=(VMEM, VMEM),
        compiler_params=PARAMS,
    )(left, *blocks)
    return density.reshape(cells), rho


def shards(coeffs, occupations, counts, intersection, phi_values, panel_values, proj_site, proj_panel):
    n_row, n_col, n_slab = (lax.axis_size(a) for a in ("prow", "pcol", "dz"))
    rows = coeffs.shape[0]
    fits = coeffs.size * 2 * n_row * n_col <= GATHER_LIMIT
    regular = n_row == 2 and n_col == 4 and n_slab == 4 and rows >= PW and rows % 256 == 0
    plan = gather_shards if fits and regular else exchange_shards
    return plan(coeffs, occupations, counts, intersection, phi_values, panel_values, proj_site, proj_panel)


def solution(mesh):
    return jax.shard_map(
        shards,
        mesh=mesh,
        in_specs=(
            P("prow", "pcol"),
            P("pcol"),
            P(),
            P(),
            P(("prow", "pcol", "dz"), None),
            P(("prow", "pcol", "dz"), None),
            P(("prow", "pcol"), None, None),
            P(("prow", "pcol"), None, "dz"),
        ),
        out_specs=(P(("prow", "pcol", "dz")), P(("prow", "pcol"), None)),
        check_vma=False,
    )
```

```python
import functools

import jax
import jax.numpy as jnp
from jax import lax
from jax.experimental import pallas as pl
from jax.experimental.pallas import tpu as pltpu
from jax.sharding import PartitionSpec as P

SLOTS = 16
LIVE = 13
NPROJ = 16
PW = 512
CAP = 2
GATHER_LIMIT = 2**21

F32 = jnp.float32
BF16 = jnp.bfloat16


def spread(block, axis, holder):
    block = jnp.where(lax.axis_index(axis) == holder, block, jnp.zeros_like(block))
    return lax.psum(block, axis)


def exchange_shards(
    coeffs, occupations, counts, intersection, phi_values, panel_values, proj_site, proj_panel
):
    n_row = lax.axis_size("prow")
    n_col = lax.axis_size("pcol")
    n_slab = lax.axis_size("dz")
    rows_blk = coeffs.shape[0]
    atoms_blk = rows_blk // SLOTS
    start_atom = lax.axis_index("prow") * atoms_blk
    block_counts = lax.dynamic_slice_in_dim(counts, start_atom, atoms_blk)
    slot_ids = lax.broadcasted_iota(jnp.int32, (atoms_blk, SLOTS), 1)
    live = (slot_ids < block_counts[:, None]).reshape(rows_blk, 1)
    masked = jnp.where(live, coeffs, jnp.zeros((), coeffs.dtype))
    weights = (occupations.astype(jnp.float32) * 0.5).astype(coeffs.dtype)
    panel = spread(coeffs[:PW], "prow", 0)
    panel_slots = lax.broadcasted_iota(jnp.int32, (PW // SLOTS, SLOTS), 1)
    panel_live = (panel_slots < counts[: PW // SLOTS][:, None]).reshape(PW, 1)
    panel = jnp.where(panel_live, panel, jnp.zeros((), panel.dtype))
    scaled = masked * weights[None, :]
    owned = lax.psum_scatter(
        lax.dot_general(
            scaled, panel, (((1,), (1,)), ((), ())), preferred_element_type=jnp.float32
        ),
        "pcol",
        scatter_dimension=0,
        tiled=True,
    )
    owned_rows = owned.astype(jnp.bfloat16)
    atoms_own = owned_rows.shape[0] // SLOTS
    owned_blocks = owned_rows.reshape(atoms_own, SLOTS, PW)
    owner_id = lax.axis_index("prow") * n_col + lax.axis_index("pcol")
    slab = lax.axis_index("dz")
    receivers = n_row * n_col
    by_slab = intersection.reshape(receivers, n_slab, intersection.shape[1])
    lists = lax.dynamic_index_in_dim(by_slab, slab, 1, keepdims=False)
    mine = lists // atoms_own == owner_id
    ranks = jnp.cumsum(mine.astype(jnp.int32), axis=1) - 1
    slot_pick = lax.broadcasted_iota(jnp.int32, (1, 1, CAP), 2)
    picked = mine[:, :, None] & (ranks[:, :, None] == slot_pick)
    local_atom = jnp.sum(jnp.where(picked, (lists - owner_id * atoms_own)[:, :, None], 0), axis=1)
    valid = jnp.any(picked, axis=1)
    outgoing = jnp.where(
        valid[:, :, None, None], owned_blocks[local_atom], jnp.zeros((), owned_rows.dtype)
    )
    incoming = lax.all_to_all(
        outgoing.reshape(receivers * CAP * SLOTS, PW),
        ("prow", "pcol"),
        split_axis=0,
        concat_axis=0,
        tiled=True,
    )
    incoming = incoming.reshape(receivers * CAP, SLOTS, PW)
    domain = owner_id * n_slab + slab
    wanted = lax.dynamic_index_in_dim(intersection, domain, 0, keepdims=False)
    wanted_owner = wanted // atoms_own
    listed = wanted.shape[0]
    same_owner = wanted_owner[:, None] == wanted_owner[None, :]
    earlier = lax.broadcasted_iota(jnp.int32, (listed, listed), 1) < lax.broadcasted_iota(
        jnp.int32, (listed, listed), 0
    )
    rank_in = jnp.sum((same_owner & earlier).astype(jnp.int32), axis=1)
    slot_of = wanted_owner * CAP + rank_in
    domain_rows = incoming[slot_of].reshape(listed * SLOTS, PW)
    mixed = jnp.dot(phi_values, domain_rows, preferred_element_type=jnp.float32)
    density = jnp.sum(mixed * panel_values.astype(jnp.float32), axis=1)
    projected = jnp.einsum(
        "aim,amn->ain", proj_site, owned_blocks, preferred_element_type=jnp.float32
    )
    slab_cols = proj_panel.shape[2]
    part_proj = lax.dynamic_slice_in_dim(projected, slab * slab_cols, slab_cols, 2)
    partial_rho = jnp.einsum(
        "ain,ajn->aij", part_proj, proj_panel.astype(jnp.float32), precision=lax.Precision.HIGHEST
    )
    rho_full = lax.psum(partial_rho, "dz")
    return (density, rho_full.reshape(atoms_own, NPROJ * NPROJ))


def iota(shape, dim):
    return lax.broadcasted_iota(jnp.int32, shape, dim)


def pick(condition):
    return jnp.where(condition, 1.0, 0.0).astype(BF16)


def take(left, right):
    return jnp.dot(left, right, preferred_element_type=F32).astype(BF16)


def packed_rows(rows):
    return rows // SLOTS * LIVE + 16


def pack_kernel(occ_ref, coeffs_ref, out_ref, occ, held, arrived):
    rows = coeffs_ref.shape[0]
    group = 16
    span = group * SLOTS
    copies = [
        pltpu.make_async_copy(
            coeffs_ref.at[pl.ds(g * span, span)], held.at[pl.ds(g * span, span)], arrived.at[g]
        )
        for g in range(rows // span)
    ]
    last = pltpu.make_async_copy(occ_ref, occ, arrived.at[rows // span])
    for copy in copies:
        copy.start()
    last.start()
    old = iota((group * LIVE, span), 1)
    slot = old & (SLOTS - 1)
    move = pick(((old >> 4) * LIVE + slot == iota((group * LIVE, span), 0)) & (slot < LIVE))
    for g, copy in enumerate(copies):
        copy.wait()
        out_ref[g * group * LIVE : (g + 1) * group * LIVE, :] = take(move, held[g * span : (g + 1) * span, :])
    last.wait()
    weights = occ[...].reshape(1, occ.shape[0]).astype(F32) * 0.5
    out_ref[rows // SLOTS * LIVE :, :] = jnp.broadcast_to(weights, (16, weights.shape[1])).astype(BF16)


def panel_map(counts_ref, packed, first=lambda t: t):
    slot = iota((SLOTS, packed), 0)
    new = iota((SLOTS, packed), 1)
    return jnp.concatenate(
        [
            pick((new == first(t) * LIVE + slot) & (slot < counts_ref[first(t)]))
            for t in range(PW // SLOTS)
        ],
        axis=0,
    )


def left_kernel(n_col, n_slab, lists_ref, counts_ref, phi_ref, panel_ref, site_ref, out_ref):
    x, z, s = lax.axis_index("prow"), lax.axis_index("pcol"), lax.axis_index("dz")
    cells, listed = phi_ref.shape[0], lists_ref.shape[1]
    packed = out_ref.shape[2]
    own = site_ref.shape[0]
    atoms_own = own // NPROJ
    blk_atoms = (packed - 16) // LIVE
    domain = (x * n_col + z) * n_slab + s
    slot = iota((SLOTS, packed), 0)
    new = iota((SLOTS, packed), 1)
    spread_lanes = pick(iota((SLOTS, own), 0) == (iota((SLOTS, own), 1) & (SLOTS - 1)))
    tiled = take(site_ref[...], spread_lanes)
    mine = (iota((own, own), 0) & (atoms_own - 1)) == (iota((own, own), 1) >> 4)
    tiled = jnp.where(mine, tiled, jnp.zeros_like(tiled))
    first = z * atoms_own
    to_own = jnp.concatenate(
        [
            pick((new == (first + a) * LIVE + slot) & (slot < counts_ref[x * blk_atoms + first + a]))
            for a in range(atoms_own)
        ],
        axis=0,
    )
    site_side = take(tiled, to_own)
    for b in range(2):
        to_listed = jnp.concatenate(
            [
                pick(
                    (new == (lists_ref[domain, p] - b * blk_atoms) * LIVE + slot)
                    & (slot < counts_ref[lists_ref[domain, p]])
                    & (new < blk_atoms * LIVE)
                )
                for p in range(listed)
            ],
            axis=0,
        )
        out_ref[b, 0:cells, :] = take(phi_ref[...], to_listed)
        out_ref[b, 2 * cells : 2 * cells + own, :] = jnp.where(x == b, site_side, jnp.zeros_like(site_side))
    out_ref[0, cells : 2 * cells, :] = take(panel_ref[...], panel_map(counts_ref, packed))
    out_ref[1, cells : 2 * cells, :] = jnp.zeros((cells, packed), BF16)


def split(values):
    high = values.astype(BF16)
    return high, (values - high.astype(F32)).astype(BF16)


ROWS_BY_ROWS = (((1,), (1,)), ((), ()))


def partial_sums(a, b, near, cells, left_ref):
    weight_row = left_ref.shape[2] - 16
    r = jnp.dot(left_ref[near], a, preferred_element_type=F32)
    r += jnp.dot(left_ref[1 - near], b, preferred_element_type=F32)
    f = a[weight_row:, :].astype(F32)[0:1]
    term = r[:cells] * f * r[cells : 2 * cells]
    half = term.shape[1] // 2
    panel = jnp.where(near == 0, a, b)
    projected = sum(
        lax.dot_general(part, panel, ROWS_BY_ROWS, preferred_element_type=F32)
        for part in split(r[2 * cells :] * f)
    )
    return term[:, :half] + term[:, half:], projected


def early_kernel(
    cells, n_slab, counts_ref, left_ref, a_ref, b_ref, c_ref, d_ref, here_ref, far_ref, term_ref, projected_ref, proj_ref
):
    x, s = lax.axis_index("prow"), lax.axis_index("dz")
    odd = (s & 1) == 1
    a = jnp.concatenate([a_ref[...], jnp.where(odd, d_ref[...], c_ref[...])], axis=1)
    b = jnp.concatenate([b_ref[...], jnp.where(odd, c_ref[...], d_ref[...])], axis=1)
    term_ref[...], projected_ref[...] = partial_sums(a, b, x, cells, left_ref)
    atoms = PW // SLOTS // n_slab
    columns = panel_map(
        counts_ref, projected_ref.shape[1], lambda t: (s ^ (t // atoms)) * atoms + t % atoms
    )
    proj_ref[...] = take(jnp.concatenate([here_ref[...], far_ref[...]], axis=1), columns)


def late_kernel(
    cells, left_ref, a_ref, b_ref, c_ref, d_ref, term_ref, projected_ref, proj_ref, density_ref, rho_ref
):
    near = lax.axis_index("prow") ^ (lax.axis_index("dz") & 1)
    a = jnp.concatenate([a_ref[...], c_ref[...]], axis=1)
    b = jnp.concatenate([b_ref[...], d_ref[...]], axis=1)
    term, projected = partial_sums(a, b, near, cells, left_ref)
    term += term_ref[...]
    projected += projected_ref[...]
    density_ref[...] = jnp.sum(term.T, axis=0, keepdims=True)
    own = proj_ref.shape[0]
    atoms = own // NPROJ
    rho = sum(
        lax.dot_general(part, proj_ref[...], ROWS_BY_ROWS, preferred_element_type=F32)
        for part in split(projected)
    )
    rho = jnp.where((iota((own, own), 0) & (atoms - 1)) == (iota((own, own), 1) >> 4), rho, 0.0)
    wide = NPROJ * NPROJ
    fold = pick((iota((own, wide), 0) & (NPROJ - 1)) == (iota((own, wide), 1) & (NPROJ - 1)))
    rows = sum(jnp.dot(part, fold, preferred_element_type=F32) for part in split(rho))
    keep = (iota((own, wide), 0) // atoms) == (iota((own, wide), 1) >> 4)
    rho_ref[...] = jnp.sum(jnp.where(keep, rows, 0.0).reshape(NPROJ, atoms, wide), axis=0)


VMEM = pl.BlockSpec(memory_space=pltpu.VMEM)
SMEM = pl.BlockSpec(memory_space=pltpu.SMEM)
HBM = pl.BlockSpec(memory_space=pltpu.HBM)
PARAMS = pltpu.CompilerParams(vmem_limit_bytes=32 * 2**20)


def gather_shards(
    coeffs, occupations, counts, intersection, phi_values, panel_values, proj_site, proj_panel
):
    n_row, n_col, n_slab = (lax.axis_size(a) for a in ("prow", "pcol", "dz"))
    axes = ("prow", "pcol", "dz")

    def move(block, target):
        pairs = []
        for i in range(n_row * n_col * n_slab):
            x, z, s = i // (n_col * n_slab), i // n_slab % n_col, i % n_slab
            tx, tz, ts = target(x, z, s)
            pairs.append((i, (tx * n_col + tz) * n_slab + ts))
        return lax.ppermute(block, axes, pairs)

    def swap(block):
        return move(block, lambda x, z, s: (x, z, s ^ 1))

    rows, states = coeffs.shape
    packed = packed_rows(rows)
    atoms_own = proj_site.shape[0]
    own = atoms_own * NPROJ
    cells = phi_values.shape[0]
    pair = jnp.concatenate([proj_panel, swap(proj_panel)], axis=2)
    far_pair = move(pair, lambda x, z, s: (x, z, s ^ 2))
    block = pl.pallas_call(
        pack_kernel,
        out_shape=jax.ShapeDtypeStruct((packed, states), BF16),
        in_specs=[HBM, HBM],
        out_specs=VMEM,
        scratch_shapes=[
            pltpu.VMEM((states,), jnp.int32),
            pltpu.VMEM((rows, states), BF16),
            pltpu.SemaphoreType.DMA((rows // 256 + 1,)),
        ],
        compiler_params=PARAMS,
    )(
        pltpu.with_memory_space_constraint(occupations, pltpu.HBM),
        pltpu.with_memory_space_constraint(coeffs, pltpu.HBM),
    )
    got = {k: move(block, lambda x, z, s: (x ^ (s & 1), z ^ k, s)) for k in (2, 3, 1)}
    other = move(block, lambda x, z, s: (x ^ 1, z, s))
    site = proj_site.transpose(1, 0, 2).reshape(own, SLOTS)
    left = pl.pallas_call(
        functools.partial(left_kernel, n_col, n_slab),
        out_shape=jax.ShapeDtypeStruct((2, 2 * cells + own, packed), BF16),
        in_specs=[SMEM, SMEM, VMEM, VMEM, VMEM],
        out_specs=VMEM,
        compiler_params=PARAMS,
        cost_estimate=pl.CostEstimate(flops=2 * 10**8, bytes_accessed=2 * 10**6, transcendentals=0),
    )(intersection, counts, phi_values, panel_values, site)
    got[2], left = lax.optimization_barrier((got[2], left))
    got[3], far_pair = lax.optimization_barrier((got[3], far_pair))
    swapped = {k: swap(got[k]) for k in got}
    early = pl.pallas_call(
        functools.partial(early_kernel, cells, n_slab),
        out_shape=(
            jax.ShapeDtypeStruct((cells, states), F32),
            jax.ShapeDtypeStruct((own, packed), F32),
            jax.ShapeDtypeStruct((own, packed), BF16),
        ),
        in_specs=[SMEM] + [VMEM] * 7,
        out_specs=(VMEM, VMEM, VMEM),
        compiler_params=PARAMS,
    )(counts, left, block, other, got[2], swapped[2], pair.reshape(own, -1), far_pair.reshape(own, -1))
    density, rho = pl.pallas_call(
        functools.partial(late_kernel, cells),
        out_shape=(
            jax.ShapeDtypeStruct((1, cells), F32),
            jax.ShapeDtypeStruct((atoms_own, NPROJ * NPROJ), F32),
        ),
        in_specs=[VMEM] * 8,
        out_specs=(VMEM, VMEM),
        compiler_params=PARAMS,
    )(left, got[3], swapped[3], got[1], swapped[1], *early)
    return density.reshape(cells), rho


def shards(coeffs, occupations, counts, intersection, phi_values, panel_values, proj_site, proj_panel):
    n_row, n_col, n_slab = (lax.axis_size(a) for a in ("prow", "pcol", "dz"))
    rows = coeffs.shape[0]
    fits = coeffs.size * 2 * n_row * n_col <= GATHER_LIMIT
    regular = n_row == 2 and n_col == 4 and n_slab == 4 and rows >= PW and rows % 256 == 0
    plan = gather_shards if fits and regular else exchange_shards
    return plan(coeffs, occupations, counts, intersection, phi_values, panel_values, proj_site, proj_panel)


def solution(mesh):
    return jax.shard_map(
        shards,
        mesh=mesh,
        in_specs=(
            P("prow", "pcol"),
            P("pcol"),
            P(),
            P(),
            P(("prow", "pcol", "dz"), None),
            P(("prow", "pcol", "dz"), None),
            P(("prow", "pcol"), None, None),
            P(("prow", "pcol"), None, "dz"),
        ),
        out_specs=(P(("prow", "pcol", "dz")), P(("prow", "pcol"), None)),
        check_vma=False,
    )
```

```python
import functools

import jax
import jax.numpy as jnp
from jax import lax
from jax.experimental import pallas as pl
from jax.experimental.pallas import tpu as pltpu
from jax.sharding import PartitionSpec as P

SLOTS = 16
LIVE = 13
NPROJ = 16
PW = 512
CAP = 2
GATHER_LIMIT = 2**21

F32 = jnp.float32
BF16 = jnp.bfloat16


def spread(block, axis, holder):
    block = jnp.where(lax.axis_index(axis) == holder, block, jnp.zeros_like(block))
    return lax.psum(block, axis)


def exchange_shards(
    coeffs, occupations, counts, intersection, phi_values, panel_values, proj_site, proj_panel
):
    n_row = lax.axis_size("prow")
    n_col = lax.axis_size("pcol")
    n_slab = lax.axis_size("dz")
    rows_blk = coeffs.shape[0]
    atoms_blk = rows_blk // SLOTS
    start_atom = lax.axis_index("prow") * atoms_blk
    block_counts = lax.dynamic_slice_in_dim(counts, start_atom, atoms_blk)
    slot_ids = lax.broadcasted_iota(jnp.int32, (atoms_blk, SLOTS), 1)
    live = (slot_ids < block_counts[:, None]).reshape(rows_blk, 1)
    masked = jnp.where(live, coeffs, jnp.zeros((), coeffs.dtype))
    weights = (occupations.astype(jnp.float32) * 0.5).astype(coeffs.dtype)
    panel = spread(coeffs[:PW], "prow", 0)
    panel_slots = lax.broadcasted_iota(jnp.int32, (PW // SLOTS, SLOTS), 1)
    panel_live = (panel_slots < counts[: PW // SLOTS][:, None]).reshape(PW, 1)
    panel = jnp.where(panel_live, panel, jnp.zeros((), panel.dtype))
    scaled = masked * weights[None, :]
    owned = lax.psum_scatter(
        lax.dot_general(
            scaled, panel, (((1,), (1,)), ((), ())), preferred_element_type=jnp.float32
        ),
        "pcol",
        scatter_dimension=0,
        tiled=True,
    )
    owned_rows = owned.astype(jnp.bfloat16)
    atoms_own = owned_rows.shape[0] // SLOTS
    owned_blocks = owned_rows.reshape(atoms_own, SLOTS, PW)
    owner_id = lax.axis_index("prow") * n_col + lax.axis_index("pcol")
    slab = lax.axis_index("dz")
    receivers = n_row * n_col
    by_slab = intersection.reshape(receivers, n_slab, intersection.shape[1])
    lists = lax.dynamic_index_in_dim(by_slab, slab, 1, keepdims=False)
    mine = lists // atoms_own == owner_id
    ranks = jnp.cumsum(mine.astype(jnp.int32), axis=1) - 1
    slot_pick = lax.broadcasted_iota(jnp.int32, (1, 1, CAP), 2)
    picked = mine[:, :, None] & (ranks[:, :, None] == slot_pick)
    local_atom = jnp.sum(jnp.where(picked, (lists - owner_id * atoms_own)[:, :, None], 0), axis=1)
    valid = jnp.any(picked, axis=1)
    outgoing = jnp.where(
        valid[:, :, None, None], owned_blocks[local_atom], jnp.zeros((), owned_rows.dtype)
    )
    incoming = lax.all_to_all(
        outgoing.reshape(receivers * CAP * SLOTS, PW),
        ("prow", "pcol"),
        split_axis=0,
        concat_axis=0,
        tiled=True,
    )
    incoming = incoming.reshape(receivers * CAP, SLOTS, PW)
    domain = owner_id * n_slab + slab
    wanted = lax.dynamic_index_in_dim(intersection, domain, 0, keepdims=False)
    wanted_owner = wanted // atoms_own
    listed = wanted.shape[0]
    same_owner = wanted_owner[:, None] == wanted_owner[None, :]
    earlier = lax.broadcasted_iota(jnp.int32, (listed, listed), 1) < lax.broadcasted_iota(
        jnp.int32, (listed, listed), 0
    )
    rank_in = jnp.sum((same_owner & earlier).astype(jnp.int32), axis=1)
    slot_of = wanted_owner * CAP + rank_in
    domain_rows = incoming[slot_of].reshape(listed * SLOTS, PW)
    mixed = jnp.dot(phi_values, domain_rows, preferred_element_type=jnp.float32)
    density = jnp.sum(mixed * panel_values.astype(jnp.float32), axis=1)
    projected = jnp.einsum(
        "aim,amn->ain", proj_site, owned_blocks, preferred_element_type=jnp.float32
    )
    slab_cols = proj_panel.shape[2]
    part_proj = lax.dynamic_slice_in_dim(projected, slab * slab_cols, slab_cols, 2)
    partial_rho = jnp.einsum(
        "ain,ajn->aij", part_proj, proj_panel.astype(jnp.float32), precision=lax.Precision.HIGHEST
    )
    rho_full = lax.psum(partial_rho, "dz")
    return (density, rho_full.reshape(atoms_own, NPROJ * NPROJ))


def iota(shape, dim):
    return lax.broadcasted_iota(jnp.int32, shape, dim)


def pick(condition):
    return jnp.where(condition, 1.0, 0.0).astype(BF16)


def take(left, right):
    return jnp.dot(left, right, preferred_element_type=F32).astype(BF16)


def packed_rows(rows):
    return rows // SLOTS * LIVE + 16


def pack_kernel(occ_ref, coeffs_ref, out_ref, occ, held, arrived):
    rows = coeffs_ref.shape[0]
    group = 16
    span = group * SLOTS
    copies = [
        pltpu.make_async_copy(
            coeffs_ref.at[pl.ds(g * span, span)], held.at[pl.ds(g * span, span)], arrived.at[g]
        )
        for g in range(rows // span)
    ]
    last = pltpu.make_async_copy(occ_ref, occ, arrived.at[rows // span])
    for copy in copies:
        copy.start()
    last.start()
    old = iota((group * LIVE, span), 1)
    slot = old & (SLOTS - 1)
    move = pick(((old >> 4) * LIVE + slot == iota((group * LIVE, span), 0)) & (slot < LIVE))
    for g, copy in enumerate(copies):
        copy.wait()
        out_ref[g * group * LIVE : (g + 1) * group * LIVE, :] = take(move, held[g * span : (g + 1) * span, :])
    last.wait()
    weights = occ[...].reshape(1, occ.shape[0]).astype(F32) * 0.5
    out_ref[rows // SLOTS * LIVE :, :] = jnp.broadcast_to(weights, (16, weights.shape[1])).astype(BF16)


def panel_map(counts_ref, packed, first=lambda t: t):
    slot = iota((SLOTS, packed), 0)
    new = iota((SLOTS, packed), 1)
    return jnp.concatenate(
        [
            pick((new == first(t) * LIVE + slot) & (slot < counts_ref[first(t)]))
            for t in range(PW // SLOTS)
        ],
        axis=0,
    )


def left_kernel(n_col, n_slab, lists_ref, counts_ref, phi_ref, panel_ref, site_ref, out_ref):
    x, z, s = lax.axis_index("prow"), lax.axis_index("pcol"), lax.axis_index("dz")
    cells, listed = phi_ref.shape[0], lists_ref.shape[1]
    packed = out_ref.shape[2]
    own = site_ref.shape[0]
    atoms_own = own // NPROJ
    blk_atoms = (packed - 16) // LIVE
    domain = (x * n_col + z) * n_slab + s
    slot = iota((SLOTS, packed), 0)
    new = iota((SLOTS, packed), 1)
    spread_lanes = pick(iota((SLOTS, own), 0) == (iota((SLOTS, own), 1) & (SLOTS - 1)))
    tiled = take(site_ref[...], spread_lanes)
    mine = (iota((own, own), 0) & (atoms_own - 1)) == (iota((own, own), 1) >> 4)
    tiled = jnp.where(mine, tiled, jnp.zeros_like(tiled))
    first = z * atoms_own
    to_own = jnp.concatenate(
        [
            pick((new == (first + a) * LIVE + slot) & (slot < counts_ref[x * blk_atoms + first + a]))
            for a in range(atoms_own)
        ],
        axis=0,
    )
    site_side = take(tiled, to_own)
    for b in range(2):
        to_listed = jnp.concatenate(
            [
                pick(
                    (new == (lists_ref[domain, p] - b * blk_atoms) * LIVE + slot)
                    & (slot < counts_ref[lists_ref[domain, p]])
                    & (new < blk_atoms * LIVE)
                )
                for p in range(listed)
            ],
            axis=0,
        )
        out_ref[b, 0:cells, :] = take(phi_ref[...], to_listed)
        out_ref[b, 2 * cells : 2 * cells + own, :] = jnp.where(x == b, site_side, jnp.zeros_like(site_side))
    out_ref[0, cells : 2 * cells, :] = take(panel_ref[...], panel_map(counts_ref, packed))
    out_ref[1, cells : 2 * cells, :] = jnp.zeros((cells, packed), BF16)


def split(values):
    high = values.astype(BF16)
    return high, (values - high.astype(F32)).astype(BF16)


def partial_sums(a, b, near, cells, left_ref, proj_ref):
    weight_row = left_ref.shape[2] - 16
    r = jnp.dot(left_ref[near], a, preferred_element_type=F32)
    r += jnp.dot(left_ref[1 - near], b, preferred_element_type=F32)
    right = jnp.dot(proj_ref[...], jnp.where(near == 0, a, b), preferred_element_type=F32)
    f = a[weight_row:, :].astype(F32)[0:1]
    term = r[:cells] * f * r[cells : 2 * cells]
    term = sum(term[:, at : at + cells] for at in range(0, term.shape[1], cells))
    high, low = split(r[2 * cells :] * f)
    right_high, right_low = split(right)
    rho = sum(
        lax.dot_general(one, two, (((1,), (1,)), ((), ())), preferred_element_type=F32)
        for one, two in ((high, right_high), (low, right_high), (high, right_low))
    )
    return term, rho


def proj_kernel(n_slab, counts_ref, here_ref, far_ref, out_ref):
    s = lax.axis_index("dz")
    atoms = PW // SLOTS // n_slab
    columns = panel_map(counts_ref, out_ref.shape[1], lambda t: (s ^ (t // atoms)) * atoms + t % atoms)
    out_ref[...] = take(jnp.concatenate([here_ref[...], far_ref[...]], axis=1), columns)


def early_kernel(cells, left_ref, proj_ref, a_ref, b_ref, c_ref, d_ref, term_ref, rho_ref):
    x, s = lax.axis_index("prow"), lax.axis_index("dz")
    odd = (s & 1) == 1
    c, d = c_ref[...], d_ref[...]
    a = jnp.concatenate([a_ref[...], jnp.where(odd, d, c)], axis=1)
    b = jnp.concatenate([b_ref[...], jnp.where(odd, c, d)], axis=1)
    term_ref[...], rho_ref[...] = partial_sums(a, b, x, cells, left_ref, proj_ref)


def late_kernel(cells, left_ref, proj_ref, a_ref, b_ref, c_ref, d_ref, term_ref, part_ref, density_ref, rho_ref):
    near = lax.axis_index("prow") ^ (lax.axis_index("dz") & 1)
    a = jnp.concatenate([a_ref[...], c_ref[...]], axis=1)
    b = jnp.concatenate([b_ref[...], d_ref[...]], axis=1)
    term, rho = partial_sums(a, b, near, cells, left_ref, proj_ref)
    term += term_ref[...]
    rho += part_ref[...]
    density_ref[...] = jnp.sum(term.T, axis=0, keepdims=True)
    own = proj_ref.shape[0]
    atoms = own // NPROJ
    rho = jnp.where((iota((own, own), 0) & (atoms - 1)) == (iota((own, own), 1) >> 4), rho, 0.0)
    wide = NPROJ * NPROJ
    fold = pick((iota((own, wide), 0) & (NPROJ - 1)) == (iota((own, wide), 1) & (NPROJ - 1)))
    rows = sum(jnp.dot(part, fold, preferred_element_type=F32) for part in split(rho))
    keep = (iota((own, wide), 0) // atoms) == (iota((own, wide), 1) >> 4)
    rho_ref[...] = jnp.sum(jnp.where(keep, rows, 0.0).reshape(NPROJ, atoms, wide), axis=0)


VMEM = pl.BlockSpec(memory_space=pltpu.VMEM)
SMEM = pl.BlockSpec(memory_space=pltpu.SMEM)
HBM = pl.BlockSpec(memory_space=pltpu.HBM)
PARAMS = pltpu.CompilerParams(vmem_limit_bytes=32 * 2**20)


def gather_shards(
    coeffs, occupations, counts, intersection, phi_values, panel_values, proj_site, proj_panel
):
    n_row, n_col, n_slab = (lax.axis_size(a) for a in ("prow", "pcol", "dz"))
    axes = ("prow", "pcol", "dz")

    def move(block, target):
        pairs = []
        for i in range(n_row * n_col * n_slab):
            x, z, s = i // (n_col * n_slab), i // n_slab % n_col, i % n_slab
            tx, tz, ts = target(x, z, s)
            pairs.append((i, (tx * n_col + tz) * n_slab + ts))
        return lax.ppermute(block, axes, pairs)

    def swap(block):
        return move(block, lambda x, z, s: (x, z, s ^ 1))

    rows, states = coeffs.shape
    packed = packed_rows(rows)
    atoms_own = proj_site.shape[0]
    own = atoms_own * NPROJ
    cells = phi_values.shape[0]
    pair = jnp.concatenate([proj_panel, swap(proj_panel)], axis=2)
    far_pair = move(pair, lambda x, z, s: (x, z, s ^ 2))
    block = pl.pallas_call(
        pack_kernel,
        out_shape=jax.ShapeDtypeStruct((packed, states), BF16),
        in_specs=[HBM, HBM],
        out_specs=VMEM,
        scratch_shapes=[
            pltpu.VMEM((states,), jnp.int32),
            pltpu.VMEM((rows, states), BF16),
            pltpu.SemaphoreType.DMA((rows // 256 + 1,)),
        ],
        compiler_params=PARAMS,
    )(
        pltpu.with_memory_space_constraint(occupations, pltpu.HBM),
        pltpu.with_memory_space_constraint(coeffs, pltpu.HBM),
    )
    got = {k: move(block, lambda x, z, s: (x ^ (s & 1), z ^ k, s)) for k in (2, 3, 1)}
    other = move(block, lambda x, z, s: (x ^ 1, z, s))
    site = proj_site.transpose(1, 0, 2).reshape(own, SLOTS)
    left = pl.pallas_call(
        functools.partial(left_kernel, n_col, n_slab),
        out_shape=jax.ShapeDtypeStruct((2, 2 * cells + own, packed), BF16),
        in_specs=[SMEM, SMEM, VMEM, VMEM, VMEM],
        out_specs=VMEM,
        compiler_params=PARAMS,
        cost_estimate=pl.CostEstimate(flops=2 * 10**8, bytes_accessed=2 * 10**6, transcendentals=0),
    )(intersection, counts, phi_values, panel_values, site)
    proj = pl.pallas_call(
        functools.partial(proj_kernel, n_slab),
        out_shape=jax.ShapeDtypeStruct((own, packed), BF16),
        in_specs=[SMEM, VMEM, VMEM],
        out_specs=VMEM,
        compiler_params=PARAMS,
    )(counts, pair.reshape(own, -1), far_pair.reshape(own, -1))
    got[3], left = lax.optimization_barrier((got[3], left))
    swapped = {3: swap(got[3])}
    got[2], proj = lax.optimization_barrier((got[2], proj))
    early = pl.pallas_call(
        functools.partial(early_kernel, cells),
        out_shape=(jax.ShapeDtypeStruct((cells, states), F32), jax.ShapeDtypeStruct((own, own), F32)),
        in_specs=[VMEM] * 6,
        out_specs=(VMEM, VMEM),
        compiler_params=PARAMS,
    )(left, proj, block, other, got[3], swapped[3])
    swapped |= {k: swap(got[k]) for k in (2, 1)}
    density, rho = pl.pallas_call(
        functools.partial(late_kernel, cells),
        out_shape=(
            jax.ShapeDtypeStruct((1, cells), F32),
            jax.ShapeDtypeStruct((atoms_own, NPROJ * NPROJ), F32),
        ),
        in_specs=[VMEM] * 8,
        out_specs=(VMEM, VMEM),
        compiler_params=PARAMS,
    )(left, proj, got[2], swapped[2], got[1], swapped[1], *early)
    return density.reshape(cells), rho


def shards(coeffs, occupations, counts, intersection, phi_values, panel_values, proj_site, proj_panel):
    n_row, n_col, n_slab = (lax.axis_size(a) for a in ("prow", "pcol", "dz"))
    rows = coeffs.shape[0]
    fits = coeffs.size * 2 * n_row * n_col <= GATHER_LIMIT
    regular = n_row == 2 and n_col == 4 and n_slab == 4 and rows >= PW and rows % 256 == 0
    plan = gather_shards if fits and regular else exchange_shards
    return plan(coeffs, occupations, counts, intersection, phi_values, panel_values, proj_site, proj_panel)


def solution(mesh):
    return jax.shard_map(
        shards,
        mesh=mesh,
        in_specs=(
            P("prow", "pcol"),
            P("pcol"),
            P(),
            P(),
            P(("prow", "pcol", "dz"), None),
            P(("prow", "pcol", "dz"), None),
            P(("prow", "pcol"), None, None),
            P(("prow", "pcol"), None, "dz"),
        ),
        out_specs=(P(("prow", "pcol", "dz")), P(("prow", "pcol"), None)),
        check_vma=False,
    )
```

```python
import functools

import jax
import jax.numpy as jnp
from jax import lax
from jax.experimental import pallas as pl
from jax.experimental.pallas import tpu as pltpu
from jax.sharding import PartitionSpec as P

SLOTS = 16
LIVE = 13
NPROJ = 16
PW = 512
CAP = 2
GATHER_LIMIT = 2**21

F32 = jnp.float32
BF16 = jnp.bfloat16


def spread(block, axis, holder):
    block = jnp.where(lax.axis_index(axis) == holder, block, jnp.zeros_like(block))
    return lax.psum(block, axis)


def exchange_shards(
    coeffs, occupations, counts, intersection, phi_values, panel_values, proj_site, proj_panel
):
    n_row = lax.axis_size("prow")
    n_col = lax.axis_size("pcol")
    n_slab = lax.axis_size("dz")
    rows_blk = coeffs.shape[0]
    atoms_blk = rows_blk // SLOTS
    start_atom = lax.axis_index("prow") * atoms_blk
    block_counts = lax.dynamic_slice_in_dim(counts, start_atom, atoms_blk)
    slot_ids = lax.broadcasted_iota(jnp.int32, (atoms_blk, SLOTS), 1)
    live = (slot_ids < block_counts[:, None]).reshape(rows_blk, 1)
    masked = jnp.where(live, coeffs, jnp.zeros((), coeffs.dtype))
    weights = (occupations.astype(jnp.float32) * 0.5).astype(coeffs.dtype)
    panel = spread(coeffs[:PW], "prow", 0)
    panel_slots = lax.broadcasted_iota(jnp.int32, (PW // SLOTS, SLOTS), 1)
    panel_live = (panel_slots < counts[: PW // SLOTS][:, None]).reshape(PW, 1)
    panel = jnp.where(panel_live, panel, jnp.zeros((), panel.dtype))
    scaled = masked * weights[None, :]
    owned = lax.psum_scatter(
        lax.dot_general(
            scaled, panel, (((1,), (1,)), ((), ())), preferred_element_type=jnp.float32
        ),
        "pcol",
        scatter_dimension=0,
        tiled=True,
    )
    owned_rows = owned.astype(jnp.bfloat16)
    atoms_own = owned_rows.shape[0] // SLOTS
    owned_blocks = owned_rows.reshape(atoms_own, SLOTS, PW)
    owner_id = lax.axis_index("prow") * n_col + lax.axis_index("pcol")
    slab = lax.axis_index("dz")
    receivers = n_row * n_col
    by_slab = intersection.reshape(receivers, n_slab, intersection.shape[1])
    lists = lax.dynamic_index_in_dim(by_slab, slab, 1, keepdims=False)
    mine = lists // atoms_own == owner_id
    ranks = jnp.cumsum(mine.astype(jnp.int32), axis=1) - 1
    slot_pick = lax.broadcasted_iota(jnp.int32, (1, 1, CAP), 2)
    picked = mine[:, :, None] & (ranks[:, :, None] == slot_pick)
    local_atom = jnp.sum(jnp.where(picked, (lists - owner_id * atoms_own)[:, :, None], 0), axis=1)
    valid = jnp.any(picked, axis=1)
    outgoing = jnp.where(
        valid[:, :, None, None], owned_blocks[local_atom], jnp.zeros((), owned_rows.dtype)
    )
    incoming = lax.all_to_all(
        outgoing.reshape(receivers * CAP * SLOTS, PW),
        ("prow", "pcol"),
        split_axis=0,
        concat_axis=0,
        tiled=True,
    )
    incoming = incoming.reshape(receivers * CAP, SLOTS, PW)
    domain = owner_id * n_slab + slab
    wanted = lax.dynamic_index_in_dim(intersection, domain, 0, keepdims=False)
    wanted_owner = wanted // atoms_own
    listed = wanted.shape[0]
    same_owner = wanted_owner[:, None] == wanted_owner[None, :]
    earlier = lax.broadcasted_iota(jnp.int32, (listed, listed), 1) < lax.broadcasted_iota(
        jnp.int32, (listed, listed), 0
    )
    rank_in = jnp.sum((same_owner & earlier).astype(jnp.int32), axis=1)
    slot_of = wanted_owner * CAP + rank_in
    domain_rows = incoming[slot_of].reshape(listed * SLOTS, PW)
    mixed = jnp.dot(phi_values, domain_rows, preferred_element_type=jnp.float32)
    density = jnp.sum(mixed * panel_values.astype(jnp.float32), axis=1)
    projected = jnp.einsum(
        "aim,amn->ain", proj_site, owned_blocks, preferred_element_type=jnp.float32
    )
    slab_cols = proj_panel.shape[2]
    part_proj = lax.dynamic_slice_in_dim(projected, slab * slab_cols, slab_cols, 2)
    partial_rho = jnp.einsum(
        "ain,ajn->aij", part_proj, proj_panel.astype(jnp.float32), precision=lax.Precision.HIGHEST
    )
    rho_full = lax.psum(partial_rho, "dz")
    return (density, rho_full.reshape(atoms_own, NPROJ * NPROJ))


def iota(shape, dim):
    return lax.broadcasted_iota(jnp.int32, shape, dim)


def pick(condition):
    return jnp.where(condition, 1.0, 0.0).astype(BF16)


def take(left, right):
    return jnp.dot(left, right, preferred_element_type=F32).astype(BF16)


def packed_rows(rows):
    return rows // SLOTS * LIVE + 16


def pack_kernel(occ_ref, coeffs_ref, out_ref, occ, held, arrived):
    rows = coeffs_ref.shape[0]
    group = 16
    span = group * SLOTS
    copies = [
        pltpu.make_async_copy(
            coeffs_ref.at[pl.ds(g * span, span)], held.at[pl.ds(g * span, span)], arrived.at[g]
        )
        for g in range(rows // span)
    ]
    last = pltpu.make_async_copy(occ_ref, occ, arrived.at[rows // span])
    for copy in copies:
        copy.start()
    last.start()
    old = iota((group * LIVE, span), 1)
    slot = old & (SLOTS - 1)
    move = pick(((old >> 4) * LIVE + slot == iota((group * LIVE, span), 0)) & (slot < LIVE))
    for g, copy in enumerate(copies):
        copy.wait()
        out_ref[g * group * LIVE : (g + 1) * group * LIVE, :] = take(move, held[g * span : (g + 1) * span, :])
    last.wait()
    weights = occ[...].reshape(1, occ.shape[0]).astype(F32) * 0.5
    out_ref[rows // SLOTS * LIVE :, :] = jnp.broadcast_to(weights, (16, weights.shape[1])).astype(BF16)


def panel_map(counts_ref, packed):
    slot = iota((SLOTS, packed), 0)
    new = iota((SLOTS, packed), 1)
    return jnp.concatenate(
        [pick((new == t * LIVE + slot) & (slot < counts_ref[t])) for t in range(PW // SLOTS)], axis=0
    )


def left_kernel(
    n_col,
    n_slab,
    lists_hbm,
    counts_hbm,
    phi_ref,
    panel_ref,
    site_ref,
    out_ref,
    columns_ref,
    lists_ref,
    counts_ref,
    arrived,
):
    copies = [
        pltpu.make_async_copy(source, target, arrived.at[i])
        for i, (source, target) in enumerate(((lists_hbm, lists_ref), (counts_hbm, counts_ref)))
    ]
    for copy in copies:
        copy.start()
    for copy in copies:
        copy.wait()
    x, z, s = lax.axis_index("prow"), lax.axis_index("pcol"), lax.axis_index("dz")
    cells, listed = phi_ref.shape[0], lists_ref.shape[0]
    packed = out_ref.shape[2]
    own = site_ref.shape[0]
    atoms_own = own // NPROJ
    blk_atoms = (packed - 16) // LIVE
    domain = (x * n_col + z) * n_slab + s
    slot = iota((SLOTS, packed), 0)
    new = iota((SLOTS, packed), 1)
    spread_lanes = pick(iota((SLOTS, own), 0) == (iota((SLOTS, own), 1) & (SLOTS - 1)))
    tiled = take(site_ref[...], spread_lanes)
    mine = (iota((own, own), 0) & (atoms_own - 1)) == (iota((own, own), 1) >> 4)
    tiled = jnp.where(mine, tiled, jnp.zeros_like(tiled))
    first = z * atoms_own
    to_own = jnp.concatenate(
        [
            pick((new == (first + a) * LIVE + slot) & (slot < counts_ref[x * blk_atoms + first + a]))
            for a in range(atoms_own)
        ],
        axis=0,
    )
    site_side = take(tiled, to_own)
    for b in range(2):
        to_listed = jnp.concatenate(
            [
                pick(
                    (new == (lists_ref[p, domain] - b * blk_atoms) * LIVE + slot)
                    & (slot < counts_ref[lists_ref[p, domain]])
                    & (new < blk_atoms * LIVE)
                )
                for p in range(listed)
            ],
            axis=0,
        )
        out_ref[b, 0:cells, :] = take(phi_ref[...], to_listed)
        out_ref[b, 2 * cells : 2 * cells + own, :] = jnp.where(x == b, site_side, jnp.zeros_like(site_side))
    columns = panel_map(counts_ref, packed)
    columns_ref[...] = columns
    out_ref[0, cells : 2 * cells, :] = take(panel_ref[...], columns)
    out_ref[1, cells : 2 * cells, :] = jnp.zeros((cells, packed), BF16)


def split(values):
    high = values.astype(BF16)
    return high, (values - high.astype(F32)).astype(BF16)


def partial_sums(a, b, near, cells, left_ref, proj_ref):
    weight_row = left_ref.shape[2] - 16
    r = jnp.dot(left_ref[near], a, preferred_element_type=F32)
    r += jnp.dot(left_ref[1 - near], b, preferred_element_type=F32)
    right = jnp.dot(proj_ref[...], jnp.where(near == 0, a, b), preferred_element_type=F32)
    f = a[weight_row:, :].astype(F32)[0:1]
    term = r[:cells] * f * r[cells : 2 * cells]
    term = sum(term[:, at : at + cells] for at in range(0, term.shape[1], cells))
    high, low = split(r[2 * cells :] * f)
    right_high, right_low = split(right)
    rho = sum(
        lax.dot_general(one, two, (((1,), (1,)), ((), ())), preferred_element_type=F32)
        for one, two in ((high, right_high), (low, right_high), (high, right_low))
    )
    return term, rho


def early_kernel(
    cells, left_ref, columns_ref, here_ref, next_ref, a_ref, b_ref, c_ref, d_ref, term_ref, rho_ref, proj_ref
):
    x, s = lax.axis_index("prow"), lax.axis_index("dz")
    odd, back = (s & 1) == 1, (s & 2) == 2
    here, after = here_ref[...], next_ref[...]
    evens, odds = jnp.where(odd, after, here), jnp.where(odd, here, after)
    half = here.shape[1] // 2
    low = [evens[:, :half], odds[:, :half]]
    high = [evens[:, half:], odds[:, half:]]
    front = [jnp.where(back, h, l) for l, h in zip(low, high)]
    rear = [jnp.where(back, l, h) for l, h in zip(low, high)]
    proj_ref[...] = take(jnp.concatenate(front + rear, axis=1), columns_ref[...])
    c, d = c_ref[...], d_ref[...]
    a = jnp.concatenate([a_ref[...], jnp.where(odd, d, c)], axis=1)
    b = jnp.concatenate([b_ref[...], jnp.where(odd, c, d)], axis=1)
    term_ref[...], rho_ref[...] = partial_sums(a, b, x, cells, left_ref, proj_ref)


def late_kernel(cells, left_ref, proj_ref, a_ref, b_ref, c_ref, d_ref, term_ref, part_ref, density_ref, rho_ref):
    near = lax.axis_index("prow") ^ (lax.axis_index("dz") & 1)
    a = jnp.concatenate([a_ref[...], c_ref[...]], axis=1)
    b = jnp.concatenate([b_ref[...], d_ref[...]], axis=1)
    term, rho = partial_sums(a, b, near, cells, left_ref, proj_ref)
    term += term_ref[...]
    rho += part_ref[...]
    density_ref[...] = jnp.sum(term.T, axis=0, keepdims=True)
    own = proj_ref.shape[0]
    atoms = own // NPROJ
    rho = jnp.where((iota((own, own), 0) & (atoms - 1)) == (iota((own, own), 1) >> 4), rho, 0.0)
    wide = NPROJ * NPROJ
    fold = pick((iota((own, wide), 0) & (NPROJ - 1)) == (iota((own, wide), 1) & (NPROJ - 1)))
    rows = sum(jnp.dot(part, fold, preferred_element_type=F32) for part in split(rho))
    keep = (iota((own, wide), 0) // atoms) == (iota((own, wide), 1) >> 4)
    rho_ref[...] = jnp.sum(jnp.where(keep, rows, 0.0).reshape(NPROJ, atoms, wide), axis=0)


VMEM = pl.BlockSpec(memory_space=pltpu.VMEM)
SMEM = pl.BlockSpec(memory_space=pltpu.SMEM)
HBM = pl.BlockSpec(memory_space=pltpu.HBM)
PARAMS = pltpu.CompilerParams(vmem_limit_bytes=32 * 2**20)


def gather_shards(
    coeffs, occupations, counts, intersection, phi_values, panel_values, proj_site, proj_panel
):
    n_row, n_col, n_slab = (lax.axis_size(a) for a in ("prow", "pcol", "dz"))
    axes = ("prow", "pcol", "dz")

    def move(block, target):
        pairs = []
        for i in range(n_row * n_col * n_slab):
            x, z, s = i // (n_col * n_slab), i // n_slab % n_col, i % n_slab
            tx, tz, ts = target(x, z, s)
            pairs.append((i, (tx * n_col + tz) * n_slab + ts))
        return lax.ppermute(block, axes, pairs)

    def swap(block):
        return move(block, lambda x, z, s: (x, z, s ^ 1))

    rows, states = coeffs.shape
    packed = packed_rows(rows)
    atoms_own = proj_site.shape[0]
    own = atoms_own * NPROJ
    cells = phi_values.shape[0]
    far = move(proj_panel, lambda x, z, s: (x, z, s ^ 2))
    block = pl.pallas_call(
        pack_kernel,
        out_shape=jax.ShapeDtypeStruct((packed, states), BF16),
        in_specs=[HBM, HBM],
        out_specs=VMEM,
        scratch_shapes=[
            pltpu.VMEM((states,), jnp.int32),
            pltpu.VMEM((rows, states), BF16),
            pltpu.SemaphoreType.DMA((rows // 256 + 1,)),
        ],
        compiler_params=PARAMS,
    )(
        pltpu.with_memory_space_constraint(occupations, pltpu.HBM),
        pltpu.with_memory_space_constraint(coeffs, pltpu.HBM),
    )
    got = {k: move(block, lambda x, z, s: (x ^ (s & 1), z ^ k, s)) for k in (1, 2, 3)}
    other = move(block, lambda x, z, s: (x ^ 1, z, s))
    site = proj_site.transpose(1, 0, 2).reshape(own, SLOTS)
    left, columns = pl.pallas_call(
        functools.partial(left_kernel, n_col, n_slab),
        out_shape=(
            jax.ShapeDtypeStruct((2, 2 * cells + own, packed), BF16),
            jax.ShapeDtypeStruct((PW, packed), BF16),
        ),
        in_specs=[HBM, HBM, VMEM, VMEM, VMEM],
        out_specs=(VMEM, VMEM),
        scratch_shapes=[
            pltpu.SMEM(intersection.shape[::-1], jnp.int32),
            pltpu.SMEM(counts.shape, jnp.int32),
            pltpu.SemaphoreType.DMA((2,)),
        ],
        compiler_params=PARAMS,
        cost_estimate=pl.CostEstimate(flops=2 * 10**8, bytes_accessed=2 * 10**6, transcendentals=0),
    )(
        pltpu.with_memory_space_constraint(intersection.T, pltpu.HBM),
        pltpu.with_memory_space_constraint(counts, pltpu.HBM),
        phi_values,
        panel_values,
        site,
    )
    far, left = lax.optimization_barrier((far, left))
    pair = jnp.concatenate([proj_panel, far], axis=2)
    next_pair = swap(pair)
    got[2], left, next_pair = lax.optimization_barrier((got[2], left, next_pair))
    swapped = {2: swap(got[2])}
    got[1], other = lax.optimization_barrier((got[1], other))
    term, rho, proj = pl.pallas_call(
        functools.partial(early_kernel, cells),
        out_shape=(
            jax.ShapeDtypeStruct((cells, states), F32),
            jax.ShapeDtypeStruct((own, own), F32),
            jax.ShapeDtypeStruct((own, packed), BF16),
        ),
        in_specs=[VMEM] * 8,
        out_specs=(VMEM, VMEM, VMEM),
        compiler_params=PARAMS,
    )(left, columns, pair.reshape(own, -1), next_pair.reshape(own, -1), block, other, got[2], swapped[2])
    swapped |= {k: swap(got[k]) for k in (1, 3)}
    density, rho = pl.pallas_call(
        functools.partial(late_kernel, cells),
        out_shape=(
            jax.ShapeDtypeStruct((1, cells), F32),
            jax.ShapeDtypeStruct((atoms_own, NPROJ * NPROJ), F32),
        ),
        in_specs=[VMEM] * 8,
        out_specs=(VMEM, VMEM),
        compiler_params=PARAMS,
    )(left, proj, got[1], swapped[1], got[3], swapped[3], term, rho)
    return density.reshape(cells), rho


def shards(coeffs, occupations, counts, intersection, phi_values, panel_values, proj_site, proj_panel):
    n_row, n_col, n_slab = (lax.axis_size(a) for a in ("prow", "pcol", "dz"))
    rows = coeffs.shape[0]
    fits = coeffs.size * 2 * n_row * n_col <= GATHER_LIMIT
    regular = n_row == 2 and n_col == 4 and n_slab == 4 and rows >= PW and rows % 256 == 0
    plan = gather_shards if fits and regular else exchange_shards
    return plan(coeffs, occupations, counts, intersection, phi_values, panel_values, proj_site, proj_panel)


def solution(mesh):
    return jax.shard_map(
        shards,
        mesh=mesh,
        in_specs=(
            P("prow", "pcol"),
            P("pcol"),
            P(),
            P(),
            P(("prow", "pcol", "dz"), None),
            P(("prow", "pcol", "dz"), None),
            P(("prow", "pcol"), None, None),
            P(("prow", "pcol"), None, "dz"),
        ),
        out_specs=(P(("prow", "pcol", "dz")), P(("prow", "pcol"), None)),
        check_vma=False,
    )
```

```python
import functools

import jax
import jax.numpy as jnp
from jax import lax
from jax.experimental import pallas as pl
from jax.experimental.pallas import tpu as pltpu
from jax.sharding import PartitionSpec as P

SLOTS = 16
LIVE = 13
NPROJ = 16
PW = 512
CAP = 2
GATHER_LIMIT = 2**21

F32 = jnp.float32
BF16 = jnp.bfloat16


def spread(block, axis, holder):
    block = jnp.where(lax.axis_index(axis) == holder, block, jnp.zeros_like(block))
    return lax.psum(block, axis)


def exchange_shards(
    coeffs, occupations, counts, intersection, phi_values, panel_values, proj_site, proj_panel
):
    n_row = lax.axis_size("prow")
    n_col = lax.axis_size("pcol")
    n_slab = lax.axis_size("dz")
    rows_blk = coeffs.shape[0]
    atoms_blk = rows_blk // SLOTS
    start_atom = lax.axis_index("prow") * atoms_blk
    block_counts = lax.dynamic_slice_in_dim(counts, start_atom, atoms_blk)
    slot_ids = lax.broadcasted_iota(jnp.int32, (atoms_blk, SLOTS), 1)
    live = (slot_ids < block_counts[:, None]).reshape(rows_blk, 1)
    masked = jnp.where(live, coeffs, jnp.zeros((), coeffs.dtype))
    weights = (occupations.astype(jnp.float32) * 0.5).astype(coeffs.dtype)
    panel = spread(coeffs[:PW], "prow", 0)
    panel_slots = lax.broadcasted_iota(jnp.int32, (PW // SLOTS, SLOTS), 1)
    panel_live = (panel_slots < counts[: PW // SLOTS][:, None]).reshape(PW, 1)
    panel = jnp.where(panel_live, panel, jnp.zeros((), panel.dtype))
    scaled = masked * weights[None, :]
    owned = lax.psum_scatter(
        lax.dot_general(
            scaled, panel, (((1,), (1,)), ((), ())), preferred_element_type=jnp.float32
        ),
        "pcol",
        scatter_dimension=0,
        tiled=True,
    )
    owned_rows = owned.astype(jnp.bfloat16)
    atoms_own = owned_rows.shape[0] // SLOTS
    owned_blocks = owned_rows.reshape(atoms_own, SLOTS, PW)
    owner_id = lax.axis_index("prow") * n_col + lax.axis_index("pcol")
    slab = lax.axis_index("dz")
    receivers = n_row * n_col
    by_slab = intersection.reshape(receivers, n_slab, intersection.shape[1])
    lists = lax.dynamic_index_in_dim(by_slab, slab, 1, keepdims=False)
    mine = lists // atoms_own == owner_id
    ranks = jnp.cumsum(mine.astype(jnp.int32), axis=1) - 1
    slot_pick = lax.broadcasted_iota(jnp.int32, (1, 1, CAP), 2)
    picked = mine[:, :, None] & (ranks[:, :, None] == slot_pick)
    local_atom = jnp.sum(jnp.where(picked, (lists - owner_id * atoms_own)[:, :, None], 0), axis=1)
    valid = jnp.any(picked, axis=1)
    outgoing = jnp.where(
        valid[:, :, None, None], owned_blocks[local_atom], jnp.zeros((), owned_rows.dtype)
    )
    incoming = lax.all_to_all(
        outgoing.reshape(receivers * CAP * SLOTS, PW),
        ("prow", "pcol"),
        split_axis=0,
        concat_axis=0,
        tiled=True,
    )
    incoming = incoming.reshape(receivers * CAP, SLOTS, PW)
    domain = owner_id * n_slab + slab
    wanted = lax.dynamic_index_in_dim(intersection, domain, 0, keepdims=False)
    wanted_owner = wanted // atoms_own
    listed = wanted.shape[0]
    same_owner = wanted_owner[:, None] == wanted_owner[None, :]
    earlier = lax.broadcasted_iota(jnp.int32, (listed, listed), 1) < lax.broadcasted_iota(
        jnp.int32, (listed, listed), 0
    )
    rank_in = jnp.sum((same_owner & earlier).astype(jnp.int32), axis=1)
    slot_of = wanted_owner * CAP + rank_in
    domain_rows = incoming[slot_of].reshape(listed * SLOTS, PW)
    mixed = jnp.dot(phi_values, domain_rows, preferred_element_type=jnp.float32)
    density = jnp.sum(mixed * panel_values.astype(jnp.float32), axis=1)
    projected = jnp.einsum(
        "aim,amn->ain", proj_site, owned_blocks, preferred_element_type=jnp.float32
    )
    slab_cols = proj_panel.shape[2]
    part_proj = lax.dynamic_slice_in_dim(projected, slab * slab_cols, slab_cols, 2)
    partial_rho = jnp.einsum(
        "ain,ajn->aij", part_proj, proj_panel.astype(jnp.float32), precision=lax.Precision.HIGHEST
    )
    rho_full = lax.psum(partial_rho, "dz")
    return (density, rho_full.reshape(atoms_own, NPROJ * NPROJ))


def iota(shape, dim):
    return lax.broadcasted_iota(jnp.int32, shape, dim)


def pick(condition):
    return jnp.where(condition, 1.0, 0.0).astype(BF16)


def take(left, right):
    return jnp.dot(left, right, preferred_element_type=F32).astype(BF16)


def packed_rows(rows):
    return rows // SLOTS * LIVE + 16


def pack_kernel(occ_ref, coeffs_ref, out_ref, half_ref, occ, held, arrived):
    rows = coeffs_ref.shape[0]
    group = 16
    span = group * SLOTS
    groups = rows // span
    copies = [
        pltpu.make_async_copy(
            coeffs_ref.at[pl.ds(g * span, span)], held.at[pl.ds(g * span, span)], arrived.at[g]
        )
        for g in range(groups)
    ]
    last = pltpu.make_async_copy(occ_ref, occ, arrived.at[groups])
    for copy in copies:
        copy.start()
    last.start()
    old = iota((group * LIVE, span), 1)
    slot = old & (SLOTS - 1)
    move = pick(((old >> 4) * LIVE + slot == iota((group * LIVE, span), 0)) & (slot < LIVE))
    tiles = []
    for g, copy in enumerate(copies):
        copy.wait()
        tiles.append(take(move, held[g * span : (g + 1) * span, :]))
        out_ref[g * group * LIVE : (g + 1) * group * LIVE, :] = tiles[-1]
    last.wait()
    weights = occ[...].reshape(1, occ.shape[0]).astype(F32) * 0.5
    weights = jnp.broadcast_to(weights, (16, weights.shape[1])).astype(BF16)
    out_ref[rows // SLOTS * LIVE :, :] = weights
    odd = (lax.axis_index("dz") & 1) == 1
    size = half_ref.shape[0] - 16
    for t in range(groups // 2):
        at = t * group * LIVE
        half_ref[at : at + group * LIVE, :] = jnp.where(odd, tiles[groups // 2 + t], tiles[t])
    half_ref[size:, :] = weights


def panel_map(counts_ref, packed):
    slot = iota((SLOTS, packed), 0)
    new = iota((SLOTS, packed), 1)
    return jnp.concatenate(
        [pick((new == t * LIVE + slot) & (slot < counts_ref[t])) for t in range(PW // SLOTS)], axis=0
    )


def left_kernel(
    n_col,
    n_slab,
    lists_hbm,
    counts_hbm,
    phi_ref,
    panel_ref,
    site_ref,
    out_ref,
    columns_ref,
    lists_ref,
    counts_ref,
    arrived,
):
    copies = [
        pltpu.make_async_copy(source, target, arrived.at[i])
        for i, (source, target) in enumerate(((lists_hbm, lists_ref), (counts_hbm, counts_ref)))
    ]
    for copy in copies:
        copy.start()
    for copy in copies:
        copy.wait()
    x, z, s = lax.axis_index("prow"), lax.axis_index("pcol"), lax.axis_index("dz")
    cells, listed = phi_ref.shape[0], lists_ref.shape[0]
    packed = out_ref.shape[2]
    own = site_ref.shape[0]
    atoms_own = own // NPROJ
    blk_atoms = (packed - 16) // LIVE
    domain = (x * n_col + z) * n_slab + s
    slot = iota((SLOTS, packed), 0)
    new = iota((SLOTS, packed), 1)
    spread_lanes = pick(iota((SLOTS, own), 0) == (iota((SLOTS, own), 1) & (SLOTS - 1)))
    tiled = take(site_ref[...], spread_lanes)
    mine = (iota((own, own), 0) & (atoms_own - 1)) == (iota((own, own), 1) >> 4)
    tiled = jnp.where(mine, tiled, jnp.zeros_like(tiled))
    first = z * atoms_own
    to_own = jnp.concatenate(
        [
            pick((new == (first + a) * LIVE + slot) & (slot < counts_ref[x * blk_atoms + first + a]))
            for a in range(atoms_own)
        ],
        axis=0,
    )
    site_side = take(tiled, to_own)
    for b in range(2):
        to_listed = jnp.concatenate(
            [
                pick(
                    (new == (lists_ref[p, domain] - b * blk_atoms) * LIVE + slot)
                    & (slot < counts_ref[lists_ref[p, domain]])
                    & (new < blk_atoms * LIVE)
                )
                for p in range(listed)
            ],
            axis=0,
        )
        out_ref[b, 0:cells, :] = take(phi_ref[...], to_listed)
        out_ref[b, 2 * cells : 2 * cells + own, :] = jnp.where(x == b, site_side, jnp.zeros_like(site_side))
    columns = panel_map(counts_ref, packed)
    columns_ref[...] = columns
    out_ref[0, cells : 2 * cells, :] = take(panel_ref[...], columns)
    out_ref[1, cells : 2 * cells, :] = jnp.zeros((cells, packed), BF16)


def split(values):
    high = values.astype(BF16)
    return high, (values - high.astype(F32)).astype(BF16)


def partial_sums(a, b, near, cells, left_ref, proj):
    weight_row = left_ref.shape[2] - 16
    r = jnp.dot(left_ref[near], a, preferred_element_type=F32)
    r += jnp.dot(left_ref[1 - near], b, preferred_element_type=F32)
    right = jnp.dot(proj, jnp.where(near == 0, a, b), preferred_element_type=F32)
    f = a[weight_row:, :].astype(F32)[0:1]
    term = r[:cells] * f * r[cells : 2 * cells]
    term = sum(term[:, at : at + cells] for at in range(0, term.shape[1], cells))
    high, low = split(r[2 * cells :] * f)
    right_high, right_low = split(right)
    rho = sum(
        lax.dot_general(one, two, (((1,), (1,)), ((), ())), preferred_element_type=F32)
        for one, two in ((high, right_high), (low, right_high), (high, right_low))
    )
    return term, rho


def sum_kernel(
    cells,
    left_ref,
    columns_ref,
    block_ref,
    other_ref,
    here_ref,
    next_ref,
    a_ref,
    b_ref,
    c_ref,
    d_ref,
    density_ref,
    rho_ref,
):
    x, s = lax.axis_index("prow"), lax.axis_index("dz")
    odd, back = (s & 1) == 1, (s & 2) == 2
    here, after = here_ref[...], next_ref[...]
    evens, odds = jnp.where(odd, after, here), jnp.where(odd, here, after)
    half = (left_ref.shape[2] - 16) // 2
    size = half + 16

    def joined(at):
        return jnp.concatenate([evens[at : at + half], odds[at : at + size]], axis=0)

    one, two = joined(0), joined(size)
    fetched = jnp.concatenate([a_ref[...], c_ref[...]], axis=1)
    swapped = jnp.concatenate([b_ref[...], d_ref[...]], axis=1)
    near = jnp.concatenate(
        [block_ref[...], jnp.where(back, two, one), jnp.where(odd, swapped, fetched)], axis=1
    )
    far = jnp.concatenate(
        [other_ref[...], jnp.where(back, one, two), jnp.where(odd, fetched, swapped)], axis=1
    )
    own = left_ref.shape[1] - 2 * cells
    last, first = 2 * size, 2 * size + own
    front = [jnp.where(back, part[last:first], part[first:]) for part in (evens, odds)]
    rear = [jnp.where(back, part[first:], part[last:first]) for part in (evens, odds)]
    proj = take(jnp.concatenate(front + rear, axis=1), columns_ref[...])
    term, rho = partial_sums(near, far, x, cells, left_ref, proj)
    density_ref[...] = jnp.sum(term.T, axis=0, keepdims=True)
    atoms = own // NPROJ
    rho = jnp.where((iota((own, own), 0) & (atoms - 1)) == (iota((own, own), 1) >> 4), rho, 0.0)
    wide = NPROJ * NPROJ
    fold = pick((iota((own, wide), 0) & (NPROJ - 1)) == (iota((own, wide), 1) & (NPROJ - 1)))
    rows = sum(jnp.dot(part, fold, preferred_element_type=F32) for part in split(rho))
    keep = (iota((own, wide), 0) // atoms) == (iota((own, wide), 1) >> 4)
    rho_ref[...] = jnp.sum(jnp.where(keep, rows, 0.0).reshape(NPROJ, atoms, wide), axis=0)


VMEM = pl.BlockSpec(memory_space=pltpu.VMEM)
HBM = pl.BlockSpec(memory_space=pltpu.HBM)
PARAMS = pltpu.CompilerParams(vmem_limit_bytes=32 * 2**20)


def gather_shards(
    coeffs, occupations, counts, intersection, phi_values, panel_values, proj_site, proj_panel
):
    n_row, n_col, n_slab = (lax.axis_size(a) for a in ("prow", "pcol", "dz"))
    axes = ("prow", "pcol", "dz")

    def move(block, target):
        pairs = []
        for i in range(n_row * n_col * n_slab):
            x, z, s = i // (n_col * n_slab), i // n_slab % n_col, i % n_slab
            tx, tz, ts = target(x, z, s)
            pairs.append((i, (tx * n_col + tz) * n_slab + ts))
        return lax.ppermute(block, axes, pairs)

    def swap(block):
        return move(block, lambda x, z, s: (x, z, s ^ 1))

    rows, states = coeffs.shape
    packed = packed_rows(rows)
    atoms_own = proj_site.shape[0]
    own = atoms_own * NPROJ
    cells = phi_values.shape[0]
    half = packed_rows(rows // 2)
    block, part = pl.pallas_call(
        pack_kernel,
        out_shape=(
            jax.ShapeDtypeStruct((packed, states), BF16),
            jax.ShapeDtypeStruct((half, states), BF16),
        ),
        in_specs=[HBM, HBM],
        out_specs=(VMEM, VMEM),
        scratch_shapes=[
            pltpu.VMEM((states,), jnp.int32),
            pltpu.VMEM((rows, states), BF16),
            pltpu.SemaphoreType.DMA((rows // 256 + 1,)),
        ],
        compiler_params=PARAMS,
    )(
        pltpu.with_memory_space_constraint(occupations, pltpu.HBM),
        pltpu.with_memory_space_constraint(coeffs, pltpu.HBM),
    )
    part = move(part, lambda x, z, s: (x ^ (s >> 1 & 1), z ^ 2, s))
    got = {k: move(block, lambda x, z, s: (x ^ (s & 1), z ^ k, s)) for k in (1, 3)}
    other = move(block, lambda x, z, s: (x ^ 1, z, s))
    site = proj_site.transpose(1, 0, 2).reshape(own, SLOTS)
    left, columns = pl.pallas_call(
        functools.partial(left_kernel, n_col, n_slab),
        out_shape=(
            jax.ShapeDtypeStruct((2, 2 * cells + own, packed), BF16),
            jax.ShapeDtypeStruct((PW, packed), BF16),
        ),
        in_specs=[HBM, HBM, VMEM, VMEM, VMEM],
        out_specs=(VMEM, VMEM),
        scratch_shapes=[
            pltpu.SMEM(intersection.shape[::-1], jnp.int32),
            pltpu.SMEM(counts.shape, jnp.int32),
            pltpu.SemaphoreType.DMA((2,)),
        ],
        compiler_params=PARAMS,
        cost_estimate=pl.CostEstimate(flops=2 * 10**8, bytes_accessed=2 * 10**6, transcendentals=0),
    )(
        pltpu.with_memory_space_constraint(intersection.T, pltpu.HBM),
        pltpu.with_memory_space_constraint(counts, pltpu.HBM),
        phi_values,
        panel_values,
        site,
    )
    projectors = proj_panel.reshape(own, -1)
    far = move(jnp.concatenate([part, projectors], axis=0), lambda x, z, s: (x, z, s ^ 2))
    other, got[3], got[1], left, far = lax.optimization_barrier((other, got[3], got[1], left, far))
    here = jnp.concatenate([part, far, projectors], axis=0)
    after = swap(here)
    swapped = {1: swap(got[1])}
    swapped[3] = swap(got[3])
    density, rho = pl.pallas_call(
        functools.partial(sum_kernel, cells),
        out_shape=(
            jax.ShapeDtypeStruct((1, cells), F32),
            jax.ShapeDtypeStruct((atoms_own, NPROJ * NPROJ), F32),
        ),
        in_specs=[VMEM] * 10,
        out_specs=(VMEM, VMEM),
        compiler_params=PARAMS,
    )(left, columns, block, other, here, after, got[1], swapped[1], got[3], swapped[3])
    return density.reshape(cells), rho


def shards(coeffs, occupations, counts, intersection, phi_values, panel_values, proj_site, proj_panel):
    n_row, n_col, n_slab = (lax.axis_size(a) for a in ("prow", "pcol", "dz"))
    rows = coeffs.shape[0]
    fits = coeffs.size * 2 * n_row * n_col <= GATHER_LIMIT
    regular = n_row == 2 and n_col == 4 and n_slab == 4 and rows >= PW and rows % 512 == 0
    plan = gather_shards if fits and regular else exchange_shards
    return plan(coeffs, occupations, counts, intersection, phi_values, panel_values, proj_site, proj_panel)


def solution(mesh):
    return jax.shard_map(
        shards,
        mesh=mesh,
        in_specs=(
            P("prow", "pcol"),
            P("pcol"),
            P(),
            P(),
            P(("prow", "pcol", "dz"), None),
            P(("prow", "pcol", "dz"), None),
            P(("prow", "pcol"), None, None),
            P(("prow", "pcol"), None, "dz"),
        ),
        out_specs=(P(("prow", "pcol", "dz")), P(("prow", "pcol"), None)),
        check_vma=False,
    )
```

```python
import functools

import jax
import jax.numpy as jnp
from jax import lax
from jax.experimental import pallas as pl
from jax.experimental.pallas import tpu as pltpu
from jax.sharding import PartitionSpec as P

SLOTS = 16
LIVE = 13
NPROJ = 16
PW = 512
CAP = 2
GATHER_LIMIT = 2**21

F32 = jnp.float32
BF16 = jnp.bfloat16


def spread(block, axis, holder):
    block = jnp.where(lax.axis_index(axis) == holder, block, jnp.zeros_like(block))
    return lax.psum(block, axis)


def exchange_shards(
    coeffs, occupations, counts, intersection, phi_values, panel_values, proj_site, proj_panel
):
    n_row = lax.axis_size("prow")
    n_col = lax.axis_size("pcol")
    n_slab = lax.axis_size("dz")
    rows_blk = coeffs.shape[0]
    atoms_blk = rows_blk // SLOTS
    start_atom = lax.axis_index("prow") * atoms_blk
    block_counts = lax.dynamic_slice_in_dim(counts, start_atom, atoms_blk)
    slot_ids = lax.broadcasted_iota(jnp.int32, (atoms_blk, SLOTS), 1)
    live = (slot_ids < block_counts[:, None]).reshape(rows_blk, 1)
    masked = jnp.where(live, coeffs, jnp.zeros((), coeffs.dtype))
    weights = (occupations.astype(jnp.float32) * 0.5).astype(coeffs.dtype)
    panel = spread(coeffs[:PW], "prow", 0)
    panel_slots = lax.broadcasted_iota(jnp.int32, (PW // SLOTS, SLOTS), 1)
    panel_live = (panel_slots < counts[: PW // SLOTS][:, None]).reshape(PW, 1)
    panel = jnp.where(panel_live, panel, jnp.zeros((), panel.dtype))
    scaled = masked * weights[None, :]
    owned = lax.psum_scatter(
        lax.dot_general(
            scaled, panel, (((1,), (1,)), ((), ())), preferred_element_type=jnp.float32
        ),
        "pcol",
        scatter_dimension=0,
        tiled=True,
    )
    owned_rows = owned.astype(jnp.bfloat16)
    atoms_own = owned_rows.shape[0] // SLOTS
    owned_blocks = owned_rows.reshape(atoms_own, SLOTS, PW)
    owner_id = lax.axis_index("prow") * n_col + lax.axis_index("pcol")
    slab = lax.axis_index("dz")
    receivers = n_row * n_col
    by_slab = intersection.reshape(receivers, n_slab, intersection.shape[1])
    lists = lax.dynamic_index_in_dim(by_slab, slab, 1, keepdims=False)
    mine = lists // atoms_own == owner_id
    ranks = jnp.cumsum(mine.astype(jnp.int32), axis=1) - 1
    slot_pick = lax.broadcasted_iota(jnp.int32, (1, 1, CAP), 2)
    picked = mine[:, :, None] & (ranks[:, :, None] == slot_pick)
    local_atom = jnp.sum(jnp.where(picked, (lists - owner_id * atoms_own)[:, :, None], 0), axis=1)
    valid = jnp.any(picked, axis=1)
    outgoing = jnp.where(
        valid[:, :, None, None], owned_blocks[local_atom], jnp.zeros((), owned_rows.dtype)
    )
    incoming = lax.all_to_all(
        outgoing.reshape(receivers * CAP * SLOTS, PW),
        ("prow", "pcol"),
        split_axis=0,
        concat_axis=0,
        tiled=True,
    )
    incoming = incoming.reshape(receivers * CAP, SLOTS, PW)
    domain = owner_id * n_slab + slab
    wanted = lax.dynamic_index_in_dim(intersection, domain, 0, keepdims=False)
    wanted_owner = wanted // atoms_own
    listed = wanted.shape[0]
    same_owner = wanted_owner[:, None] == wanted_owner[None, :]
    earlier = lax.broadcasted_iota(jnp.int32, (listed, listed), 1) < lax.broadcasted_iota(
        jnp.int32, (listed, listed), 0
    )
    rank_in = jnp.sum((same_owner & earlier).astype(jnp.int32), axis=1)
    slot_of = wanted_owner * CAP + rank_in
    domain_rows = incoming[slot_of].reshape(listed * SLOTS, PW)
    mixed = jnp.dot(phi_values, domain_rows, preferred_element_type=jnp.float32)
    density = jnp.sum(mixed * panel_values.astype(jnp.float32), axis=1)
    projected = jnp.einsum(
        "aim,amn->ain", proj_site, owned_blocks, preferred_element_type=jnp.float32
    )
    slab_cols = proj_panel.shape[2]
    part_proj = lax.dynamic_slice_in_dim(projected, slab * slab_cols, slab_cols, 2)
    partial_rho = jnp.einsum(
        "ain,ajn->aij", part_proj, proj_panel.astype(jnp.float32), precision=lax.Precision.HIGHEST
    )
    rho_full = lax.psum(partial_rho, "dz")
    return (density, rho_full.reshape(atoms_own, NPROJ * NPROJ))


def iota(shape, dim):
    return lax.broadcasted_iota(jnp.int32, shape, dim)


def pick(condition):
    return jnp.where(condition, 1.0, 0.0).astype(BF16)


def take(left, right):
    return jnp.dot(left, right, preferred_element_type=F32).astype(BF16)


def packed_rows(rows):
    return rows // SLOTS * LIVE + 16


def pack_kernel(occ_ref, coeffs_ref, out_ref, half_ref, occ, held, arrived):
    rows = coeffs_ref.shape[0]
    group = 16
    span = group * SLOTS
    groups = rows // span
    copies = [
        pltpu.make_async_copy(coeffs_ref, held, arrived.at[0]),
        pltpu.make_async_copy(occ_ref, occ, arrived.at[1]),
    ]
    for copy in copies:
        copy.start()
    old = iota((group * LIVE, span), 1)
    slot = old & (SLOTS - 1)
    move = pick(((old >> 4) * LIVE + slot == iota((group * LIVE, span), 0)) & (slot < LIVE))
    tiles = []
    for copy in copies:
        copy.wait()
    for g in range(groups):
        tiles.append(take(move, held[g * span : (g + 1) * span, :]))
        out_ref[g * group * LIVE : (g + 1) * group * LIVE, :] = tiles[-1]
    weights = occ[...].reshape(1, occ.shape[0]).astype(F32) * 0.5
    weights = jnp.broadcast_to(weights, (16, weights.shape[1])).astype(BF16)
    out_ref[rows // SLOTS * LIVE :, :] = weights
    odd = (lax.axis_index("dz") & 1) == 1
    size = half_ref.shape[0] - 16
    for t in range(groups // 2):
        at = t * group * LIVE
        half_ref[at : at + group * LIVE, :] = jnp.where(odd, tiles[groups // 2 + t], tiles[t])
    half_ref[size:, :] = weights


def panel_map(counts_ref, packed):
    slot = iota((SLOTS, packed), 0)
    new = iota((SLOTS, packed), 1)
    return jnp.concatenate(
        [pick((new == t * LIVE + slot) & (slot < counts_ref[t])) for t in range(PW // SLOTS)], axis=0
    )


def left_kernel(
    n_col,
    n_slab,
    lists_hbm,
    counts_hbm,
    phi_ref,
    panel_ref,
    site_ref,
    out_ref,
    columns_ref,
    lists_ref,
    counts_ref,
    arrived,
):
    copies = [
        pltpu.make_async_copy(source, target, arrived.at[i])
        for i, (source, target) in enumerate(((lists_hbm, lists_ref), (counts_hbm, counts_ref)))
    ]
    for copy in copies:
        copy.start()
    for copy in copies:
        copy.wait()
    x, z, s = lax.axis_index("prow"), lax.axis_index("pcol"), lax.axis_index("dz")
    cells, listed = phi_ref.shape[0], lists_ref.shape[0]
    packed = out_ref.shape[2]
    own = site_ref.shape[0]
    atoms_own = own // NPROJ
    blk_atoms = (packed - 16) // LIVE
    domain = (x * n_col + z) * n_slab + s
    slot = iota((SLOTS, packed), 0)
    new = iota((SLOTS, packed), 1)
    spread_lanes = pick(iota((SLOTS, own), 0) == (iota((SLOTS, own), 1) & (SLOTS - 1)))
    tiled = take(site_ref[...], spread_lanes)
    mine = (iota((own, own), 0) & (atoms_own - 1)) == (iota((own, own), 1) >> 4)
    tiled = jnp.where(mine, tiled, jnp.zeros_like(tiled))
    first = z * atoms_own
    to_own = jnp.concatenate(
        [
            pick((new == (first + a) * LIVE + slot) & (slot < counts_ref[x * blk_atoms + first + a]))
            for a in range(atoms_own)
        ],
        axis=0,
    )
    site_side = take(tiled, to_own)
    for b in range(2):
        to_listed = jnp.concatenate(
            [
                pick(
                    (new == (lists_ref[p, domain] - b * blk_atoms) * LIVE + slot)
                    & (slot < counts_ref[lists_ref[p, domain]])
                    & (new < blk_atoms * LIVE)
                )
                for p in range(listed)
            ],
            axis=0,
        )
        out_ref[b, 0:cells, :] = take(phi_ref[...], to_listed)
        out_ref[b, 2 * cells : 2 * cells + own, :] = jnp.where(x == b, site_side, jnp.zeros_like(site_side))
    columns = panel_map(counts_ref, packed)
    columns_ref[...] = columns
    out_ref[0, cells : 2 * cells, :] = take(panel_ref[...], columns)
    out_ref[1, cells : 2 * cells, :] = jnp.zeros((cells, packed), BF16)


def split(values):
    high = values.astype(BF16)
    return high, (values - high.astype(F32)).astype(BF16)


def partial_sums(a, b, near, cells, left_ref, proj):
    weight_row = left_ref.shape[2] - 16
    r = jnp.dot(left_ref[near], a, preferred_element_type=F32)
    r += jnp.dot(left_ref[1 - near], b, preferred_element_type=F32)
    right = jnp.dot(proj, jnp.where(near == 0, a, b), preferred_element_type=F32)
    f = a[weight_row:, :].astype(F32)[0:1]
    term = r[:cells] * f * r[cells : 2 * cells]
    term = sum(term[:, at : at + cells] for at in range(0, term.shape[1], cells))
    high, low = split(r[2 * cells :] * f)
    right_high, right_low = split(right)
    rho = sum(
        lax.dot_general(one, two, (((1,), (1,)), ((), ())), preferred_element_type=F32)
        for one, two in ((high, right_high), (low, right_high), (high, right_low))
    )
    return term, rho


def sum_kernel(
    cells,
    left_ref,
    columns_ref,
    block_ref,
    other_ref,
    here_ref,
    next_ref,
    a_ref,
    b_ref,
    c_ref,
    d_ref,
    density_ref,
    rho_ref,
):
    x, s = lax.axis_index("prow"), lax.axis_index("dz")
    odd, back = (s & 1) == 1, (s & 2) == 2
    here, after = here_ref[...], next_ref[...]
    evens, odds = jnp.where(odd, after, here), jnp.where(odd, here, after)
    half = (left_ref.shape[2] - 16) // 2
    size = half + 16

    def joined(at):
        return jnp.concatenate([evens[at : at + half], odds[at : at + size]], axis=0)

    one, two = joined(0), joined(size)
    fetched = jnp.concatenate([a_ref[...], c_ref[...]], axis=1)
    swapped = jnp.concatenate([b_ref[...], d_ref[...]], axis=1)
    near = jnp.concatenate(
        [block_ref[...], jnp.where(back, two, one), jnp.where(odd, swapped, fetched)], axis=1
    )
    far = jnp.concatenate(
        [other_ref[...], jnp.where(back, one, two), jnp.where(odd, fetched, swapped)], axis=1
    )
    own = left_ref.shape[1] - 2 * cells
    last, first = 2 * size, 2 * size + own
    front = [jnp.where(back, part[last:first], part[first:]) for part in (evens, odds)]
    rear = [jnp.where(back, part[first:], part[last:first]) for part in (evens, odds)]
    proj = take(jnp.concatenate(front + rear, axis=1), columns_ref[...])
    term, rho = partial_sums(near, far, x, cells, left_ref, proj)
    density_ref[...] = jnp.sum(term.T, axis=0, keepdims=True)
    atoms = own // NPROJ
    rho = jnp.where((iota((own, own), 0) & (atoms - 1)) == (iota((own, own), 1) >> 4), rho, 0.0)
    wide = NPROJ * NPROJ
    fold = pick((iota((own, wide), 0) & (NPROJ - 1)) == (iota((own, wide), 1) & (NPROJ - 1)))
    rows = sum(jnp.dot(part, fold, preferred_element_type=F32) for part in split(rho))
    keep = (iota((own, wide), 0) // atoms) == (iota((own, wide), 1) >> 4)
    rho_ref[...] = jnp.sum(jnp.where(keep, rows, 0.0).reshape(NPROJ, atoms, wide), axis=0)


VMEM = pl.BlockSpec(memory_space=pltpu.VMEM)
HBM = pl.BlockSpec(memory_space=pltpu.HBM)
PARAMS = pltpu.CompilerParams(vmem_limit_bytes=32 * 2**20)


def gather_shards(
    coeffs, occupations, counts, intersection, phi_values, panel_values, proj_site, proj_panel
):
    n_row, n_col, n_slab = (lax.axis_size(a) for a in ("prow", "pcol", "dz"))
    axes = ("prow", "pcol", "dz")

    def move(block, target):
        pairs = []
        for i in range(n_row * n_col * n_slab):
            x, z, s = i // (n_col * n_slab), i // n_slab % n_col, i % n_slab
            tx, tz, ts = target(x, z, s)
            pairs.append((i, (tx * n_col + tz) * n_slab + ts))
        return lax.ppermute(block, axes, pairs)

    def swap(block):
        return move(block, lambda x, z, s: (x, z, s ^ 1))

    rows, states = coeffs.shape
    packed = packed_rows(rows)
    atoms_own = proj_site.shape[0]
    own = atoms_own * NPROJ
    cells = phi_values.shape[0]
    half = packed_rows(rows // 2)
    block, part = pl.pallas_call(
        pack_kernel,
        out_shape=(
            jax.ShapeDtypeStruct((packed, states), BF16),
            jax.ShapeDtypeStruct((half, states), BF16),
        ),
        in_specs=[HBM, HBM],
        out_specs=(VMEM, VMEM),
        scratch_shapes=[
            pltpu.VMEM((states,), jnp.int32),
            pltpu.VMEM((rows, states), BF16),
            pltpu.SemaphoreType.DMA((2,)),
        ],
        compiler_params=PARAMS,
    )(
        pltpu.with_memory_space_constraint(occupations, pltpu.HBM),
        pltpu.with_memory_space_constraint(coeffs, pltpu.HBM),
    )
    part = move(part, lambda x, z, s: (x ^ (s >> 1 & 1), z ^ 2, s))
    got = {k: move(block, lambda x, z, s: (x ^ (s & 1), z ^ k, s)) for k in (1, 3)}
    other = move(block, lambda x, z, s: (x ^ 1, z, s))
    site = proj_site.transpose(1, 0, 2).reshape(own, SLOTS)
    left, columns = pl.pallas_call(
        functools.partial(left_kernel, n_col, n_slab),
        out_shape=(
            jax.ShapeDtypeStruct((2, 2 * cells + own, packed), BF16),
            jax.ShapeDtypeStruct((PW, packed), BF16),
        ),
        in_specs=[HBM, HBM, VMEM, VMEM, VMEM],
        out_specs=(VMEM, VMEM),
        scratch_shapes=[
            pltpu.SMEM(intersection.shape[::-1], jnp.int32),
            pltpu.SMEM(counts.shape, jnp.int32),
            pltpu.SemaphoreType.DMA((2,)),
        ],
        compiler_params=PARAMS,
        cost_estimate=pl.CostEstimate(flops=2 * 10**8, bytes_accessed=2 * 10**6, transcendentals=0),
    )(
        pltpu.with_memory_space_constraint(intersection.T, pltpu.HBM),
        pltpu.with_memory_space_constraint(counts, pltpu.HBM),
        phi_values,
        panel_values,
        site,
    )
    projectors = proj_panel.reshape(own, -1)
    far = move(jnp.concatenate([part, projectors], axis=0), lambda x, z, s: (x, z, s ^ 2))
    other, got[3], got[1], left, far = lax.optimization_barrier((other, got[3], got[1], left, far))
    here = jnp.concatenate([part, far, projectors], axis=0)
    after = swap(here)
    swapped = {1: swap(got[1])}
    swapped[3] = swap(got[3])
    density, rho = pl.pallas_call(
        functools.partial(sum_kernel, cells),
        out_shape=(
            jax.ShapeDtypeStruct((1, cells), F32),
            jax.ShapeDtypeStruct((atoms_own, NPROJ * NPROJ), F32),
        ),
        in_specs=[VMEM] * 10,
        out_specs=(VMEM, VMEM),
        compiler_params=PARAMS,
    )(left, columns, block, other, here, after, got[1], swapped[1], got[3], swapped[3])
    return density.reshape(cells), rho


def shards(coeffs, occupations, counts, intersection, phi_values, panel_values, proj_site, proj_panel):
    n_row, n_col, n_slab = (lax.axis_size(a) for a in ("prow", "pcol", "dz"))
    rows = coeffs.shape[0]
    fits = coeffs.size * 2 * n_row * n_col <= GATHER_LIMIT
    regular = n_row == 2 and n_col == 4 and n_slab == 4 and rows >= PW and rows % 512 == 0
    plan = gather_shards if fits and regular else exchange_shards
    return plan(coeffs, occupations, counts, intersection, phi_values, panel_values, proj_site, proj_panel)


def solution(mesh):
    return jax.shard_map(
        shards,
        mesh=mesh,
        in_specs=(
            P("prow", "pcol"),
            P("pcol"),
            P(),
            P(),
            P(("prow", "pcol", "dz"), None),
            P(("prow", "pcol", "dz"), None),
            P(("prow", "pcol"), None, None),
            P(("prow", "pcol"), None, "dz"),
        ),
        out_specs=(P(("prow", "pcol", "dz")), P(("prow", "pcol"), None)),
        check_vma=False,
    )
```

```python
import functools

import jax
import jax.numpy as jnp
from jax import lax
from jax.experimental import pallas as pl
from jax.experimental.pallas import tpu as pltpu
from jax.sharding import PartitionSpec as P

SLOTS = 16
LIVE = 13
NPROJ = 16
PW = 512
CAP = 2
GATHER_LIMIT = 2**21

F32 = jnp.float32
BF16 = jnp.bfloat16


def spread(block, axis, holder):
    block = jnp.where(lax.axis_index(axis) == holder, block, jnp.zeros_like(block))
    return lax.psum(block, axis)


def exchange_shards(
    coeffs, occupations, counts, intersection, phi_values, panel_values, proj_site, proj_panel
):
    n_row = lax.axis_size("prow")
    n_col = lax.axis_size("pcol")
    n_slab = lax.axis_size("dz")
    rows_blk = coeffs.shape[0]
    atoms_blk = rows_blk // SLOTS
    start_atom = lax.axis_index("prow") * atoms_blk
    block_counts = lax.dynamic_slice_in_dim(counts, start_atom, atoms_blk)
    slot_ids = lax.broadcasted_iota(jnp.int32, (atoms_blk, SLOTS), 1)
    live = (slot_ids < block_counts[:, None]).reshape(rows_blk, 1)
    masked = jnp.where(live, coeffs, jnp.zeros((), coeffs.dtype))
    weights = (occupations.astype(jnp.float32) * 0.5).astype(coeffs.dtype)
    panel = spread(coeffs[:PW], "prow", 0)
    panel_slots = lax.broadcasted_iota(jnp.int32, (PW // SLOTS, SLOTS), 1)
    panel_live = (panel_slots < counts[: PW // SLOTS][:, None]).reshape(PW, 1)
    panel = jnp.where(panel_live, panel, jnp.zeros((), panel.dtype))
    scaled = masked * weights[None, :]
    owned = lax.psum_scatter(
        lax.dot_general(
            scaled, panel, (((1,), (1,)), ((), ())), preferred_element_type=jnp.float32
        ),
        "pcol",
        scatter_dimension=0,
        tiled=True,
    )
    owned_rows = owned.astype(jnp.bfloat16)
    atoms_own = owned_rows.shape[0] // SLOTS
    owned_blocks = owned_rows.reshape(atoms_own, SLOTS, PW)
    owner_id = lax.axis_index("prow") * n_col + lax.axis_index("pcol")
    slab = lax.axis_index("dz")
    receivers = n_row * n_col
    by_slab = intersection.reshape(receivers, n_slab, intersection.shape[1])
    lists = lax.dynamic_index_in_dim(by_slab, slab, 1, keepdims=False)
    mine = lists // atoms_own == owner_id
    ranks = jnp.cumsum(mine.astype(jnp.int32), axis=1) - 1
    slot_pick = lax.broadcasted_iota(jnp.int32, (1, 1, CAP), 2)
    picked = mine[:, :, None] & (ranks[:, :, None] == slot_pick)
    local_atom = jnp.sum(jnp.where(picked, (lists - owner_id * atoms_own)[:, :, None], 0), axis=1)
    valid = jnp.any(picked, axis=1)
    outgoing = jnp.where(
        valid[:, :, None, None], owned_blocks[local_atom], jnp.zeros((), owned_rows.dtype)
    )
    incoming = lax.all_to_all(
        outgoing.reshape(receivers * CAP * SLOTS, PW),
        ("prow", "pcol"),
        split_axis=0,
        concat_axis=0,
        tiled=True,
    )
    incoming = incoming.reshape(receivers * CAP, SLOTS, PW)
    domain = owner_id * n_slab + slab
    wanted = lax.dynamic_index_in_dim(intersection, domain, 0, keepdims=False)
    wanted_owner = wanted // atoms_own
    listed = wanted.shape[0]
    same_owner = wanted_owner[:, None] == wanted_owner[None, :]
    earlier = lax.broadcasted_iota(jnp.int32, (listed, listed), 1) < lax.broadcasted_iota(
        jnp.int32, (listed, listed), 0
    )
    rank_in = jnp.sum((same_owner & earlier).astype(jnp.int32), axis=1)
    slot_of = wanted_owner * CAP + rank_in
    domain_rows = incoming[slot_of].reshape(listed * SLOTS, PW)
    mixed = jnp.dot(phi_values, domain_rows, preferred_element_type=jnp.float32)
    density = jnp.sum(mixed * panel_values.astype(jnp.float32), axis=1)
    projected = jnp.einsum(
        "aim,amn->ain", proj_site, owned_blocks, preferred_element_type=jnp.float32
    )
    slab_cols = proj_panel.shape[2]
    part_proj = lax.dynamic_slice_in_dim(projected, slab * slab_cols, slab_cols, 2)
    partial_rho = jnp.einsum(
        "ain,ajn->aij", part_proj, proj_panel.astype(jnp.float32), precision=lax.Precision.HIGHEST
    )
    rho_full = lax.psum(partial_rho, "dz")
    return (density, rho_full.reshape(atoms_own, NPROJ * NPROJ))


def iota(shape, dim):
    return lax.broadcasted_iota(jnp.int32, shape, dim)


def pick(condition):
    return jnp.where(condition, 1.0, 0.0).astype(BF16)


def take(left, right):
    return jnp.dot(left, right, preferred_element_type=F32).astype(BF16)


def packed_rows(rows):
    return rows // SLOTS * LIVE + 16


def pack_kernel(occ_ref, coeffs_ref, out_ref, half_ref, occ, held, arrived):
    rows = coeffs_ref.shape[0]
    group = 16
    span = group * SLOTS
    groups = rows // span
    copies = [
        pltpu.make_async_copy(coeffs_ref, held, arrived.at[0]),
        pltpu.make_async_copy(occ_ref, occ, arrived.at[1]),
    ]
    for copy in copies:
        copy.start()
    old = iota((group * LIVE, span), 1)
    slot = old & (SLOTS - 1)
    move = pick(((old >> 4) * LIVE + slot == iota((group * LIVE, span), 0)) & (slot < LIVE))
    tiles = []
    for copy in copies:
        copy.wait()
    for g in range(groups):
        tiles.append(take(move, held[g * span : (g + 1) * span, :]))
        out_ref[g * group * LIVE : (g + 1) * group * LIVE, :] = tiles[-1]
    weights = occ[...].reshape(1, occ.shape[0]).astype(F32) * 0.5
    weights = jnp.broadcast_to(weights, (16, weights.shape[1])).astype(BF16)
    out_ref[rows // SLOTS * LIVE :, :] = weights
    odd = (lax.axis_index("dz") & 1) == 1
    size = half_ref.shape[0] - 16
    for t in range(groups // 2):
        at = t * group * LIVE
        half_ref[at : at + group * LIVE, :] = jnp.where(odd, tiles[groups // 2 + t], tiles[t])
    half_ref[size:, :] = weights


def panel_map(counts_ref, packed):
    slot = iota((SLOTS, packed), 0)
    new = iota((SLOTS, packed), 1)
    return jnp.concatenate(
        [pick((new == t * LIVE + slot) & (slot < counts_ref[t])) for t in range(PW // SLOTS)], axis=0
    )


def left_kernel(
    n_col,
    n_slab,
    lists_hbm,
    counts_hbm,
    phi_ref,
    panel_ref,
    site_ref,
    out_ref,
    columns_ref,
    lists_ref,
    counts_ref,
    arrived,
):
    copies = [
        pltpu.make_async_copy(source, target, arrived.at[i])
        for i, (source, target) in enumerate(((lists_hbm, lists_ref), (counts_hbm, counts_ref)))
    ]
    for copy in copies:
        copy.start()
    for copy in copies:
        copy.wait()
    x, z, s = lax.axis_index("prow"), lax.axis_index("pcol"), lax.axis_index("dz")
    cells, listed = phi_ref.shape[0], lists_ref.shape[0]
    packed = out_ref.shape[2]
    own = site_ref.shape[0]
    atoms_own = own // NPROJ
    blk_atoms = (packed - 16) // LIVE
    domain = (x * n_col + z) * n_slab + s
    slot = iota((SLOTS, packed), 0)
    new = iota((SLOTS, packed), 1)
    spread_lanes = pick(iota((SLOTS, own), 0) == (iota((SLOTS, own), 1) & (SLOTS - 1)))
    tiled = take(site_ref[...], spread_lanes)
    mine = (iota((own, own), 0) & (atoms_own - 1)) == (iota((own, own), 1) >> 4)
    tiled = jnp.where(mine, tiled, jnp.zeros_like(tiled))
    first = z * atoms_own
    to_own = jnp.concatenate(
        [
            pick((new == (first + a) * LIVE + slot) & (slot < counts_ref[x * blk_atoms + first + a]))
            for a in range(atoms_own)
        ],
        axis=0,
    )
    site_side = take(tiled, to_own)
    for b in range(2):
        to_listed = jnp.concatenate(
            [
                pick(
                    (new == (lists_ref[p, domain] - b * blk_atoms) * LIVE + slot)
                    & (slot < counts_ref[lists_ref[p, domain]])
                    & (new < blk_atoms * LIVE)
                )
                for p in range(listed)
            ],
            axis=0,
        )
        out_ref[b, 0:cells, :] = take(phi_ref[...], to_listed)
        out_ref[b, 2 * cells : 2 * cells + own, :] = jnp.where(x == b, site_side, jnp.zeros_like(site_side))
    columns = panel_map(counts_ref, packed)
    columns_ref[...] = columns
    out_ref[0, cells : 2 * cells, :] = take(panel_ref[...], columns)
    out_ref[1, cells : 2 * cells, :] = jnp.zeros((cells, packed), BF16)


def split(values):
    high = values.astype(BF16)
    return high, (values - high.astype(F32)).astype(BF16)


def partial_sums(a, b, near, cells, left_ref, proj):
    weight_row = left_ref.shape[2] - 16
    panel, rest = jnp.where(near == 0, a, b), jnp.where(near == 0, b, a)
    r = jnp.dot(left_ref[0], panel, preferred_element_type=F32)
    right = jnp.dot(proj, panel, preferred_element_type=F32)
    listed = r[:cells] + jnp.dot(left_ref[1, :cells], rest, preferred_element_type=F32)
    atoms = r[2 * cells :] + jnp.dot(left_ref[1, 2 * cells :], rest, preferred_element_type=F32)
    f = a[weight_row:, :].astype(F32)[0:1]
    term = listed * f * r[cells : 2 * cells]
    term = sum(term[:, at : at + cells] for at in range(0, term.shape[1], cells))
    high, low = split(atoms * f)
    right_high, right_low = split(right)
    rho = sum(
        lax.dot_general(one, two, (((1,), (1,)), ((), ())), preferred_element_type=F32)
        for one, two in ((high, right_high), (low, right_high), (high, right_low))
    )
    return term, rho


def sum_kernel(
    cells,
    left_ref,
    columns_ref,
    block_ref,
    other_ref,
    here_ref,
    next_ref,
    a_ref,
    b_ref,
    c_ref,
    d_ref,
    density_ref,
    rho_ref,
):
    x, s = lax.axis_index("prow"), lax.axis_index("dz")
    odd, back = (s & 1) == 1, (s & 2) == 2
    here, after = here_ref[...], next_ref[...]
    evens, odds = jnp.where(odd, after, here), jnp.where(odd, here, after)
    half = (left_ref.shape[2] - 16) // 2
    size = half + 16

    def joined(at):
        return jnp.concatenate([evens[at : at + half], odds[at : at + size]], axis=0)

    one, two = joined(0), joined(size)
    fetched = jnp.concatenate([a_ref[...], c_ref[...]], axis=1)
    swapped = jnp.concatenate([b_ref[...], d_ref[...]], axis=1)
    near = jnp.concatenate(
        [block_ref[...], jnp.where(back, two, one), jnp.where(odd, swapped, fetched)], axis=1
    )
    far = jnp.concatenate(
        [other_ref[...], jnp.where(back, one, two), jnp.where(odd, fetched, swapped)], axis=1
    )
    own = left_ref.shape[1] - 2 * cells
    last, first = 2 * size, 2 * size + own
    front = [jnp.where(back, part[last:first], part[first:]) for part in (evens, odds)]
    rear = [jnp.where(back, part[first:], part[last:first]) for part in (evens, odds)]
    proj = take(jnp.concatenate(front + rear, axis=1), columns_ref[...])
    term, rho = partial_sums(near, far, x, cells, left_ref, proj)
    density_ref[...] = jnp.sum(term.T, axis=0, keepdims=True)
    atoms = own // NPROJ
    rho = jnp.where((iota((own, own), 0) & (atoms - 1)) == (iota((own, own), 1) >> 4), rho, 0.0)
    wide = NPROJ * NPROJ
    fold = pick((iota((own, wide), 0) & (NPROJ - 1)) == (iota((own, wide), 1) & (NPROJ - 1)))
    rows = sum(jnp.dot(part, fold, preferred_element_type=F32) for part in split(rho))
    keep = (iota((own, wide), 0) // atoms) == (iota((own, wide), 1) >> 4)
    rho_ref[...] = jnp.sum(jnp.where(keep, rows, 0.0).reshape(NPROJ, atoms, wide), axis=0)


VMEM = pl.BlockSpec(memory_space=pltpu.VMEM)
HBM = pl.BlockSpec(memory_space=pltpu.HBM)
PARAMS = pltpu.CompilerParams(vmem_limit_bytes=32 * 2**20)


def gather_shards(
    coeffs, occupations, counts, intersection, phi_values, panel_values, proj_site, proj_panel
):
    n_row, n_col, n_slab = (lax.axis_size(a) for a in ("prow", "pcol", "dz"))
    axes = ("prow", "pcol", "dz")

    def move(block, target):
        pairs = []
        for i in range(n_row * n_col * n_slab):
            x, z, s = i // (n_col * n_slab), i // n_slab % n_col, i % n_slab
            tx, tz, ts = target(x, z, s)
            pairs.append((i, (tx * n_col + tz) * n_slab + ts))
        return lax.ppermute(block, axes, pairs)

    def swap(block):
        return move(block, lambda x, z, s: (x, z, s ^ 1))

    rows, states = coeffs.shape
    packed = packed_rows(rows)
    atoms_own = proj_site.shape[0]
    own = atoms_own * NPROJ
    cells = phi_values.shape[0]
    half = packed_rows(rows // 2)
    block, part = pl.pallas_call(
        pack_kernel,
        out_shape=(
            jax.ShapeDtypeStruct((packed, states), BF16),
            jax.ShapeDtypeStruct((half, states), BF16),
        ),
        in_specs=[HBM, HBM],
        out_specs=(VMEM, VMEM),
        scratch_shapes=[
            pltpu.VMEM((states,), jnp.int32),
            pltpu.VMEM((rows, states), BF16),
            pltpu.SemaphoreType.DMA((2,)),
        ],
        compiler_params=PARAMS,
    )(
        pltpu.with_memory_space_constraint(occupations, pltpu.HBM),
        pltpu.with_memory_space_constraint(coeffs, pltpu.HBM),
    )
    part = move(part, lambda x, z, s: (x ^ (s >> 1 & 1), z ^ 2, s))
    got = {k: move(block, lambda x, z, s: (x ^ (s & 1), z ^ k, s)) for k in (1, 3)}
    other = move(block, lambda x, z, s: (x ^ 1, z, s))
    site = proj_site.transpose(1, 0, 2).reshape(own, SLOTS)
    left, columns = pl.pallas_call(
        functools.partial(left_kernel, n_col, n_slab),
        out_shape=(
            jax.ShapeDtypeStruct((2, 2 * cells + own, packed), BF16),
            jax.ShapeDtypeStruct((PW, packed), BF16),
        ),
        in_specs=[HBM, HBM, VMEM, VMEM, VMEM],
        out_specs=(VMEM, VMEM),
        scratch_shapes=[
            pltpu.SMEM(intersection.shape[::-1], jnp.int32),
            pltpu.SMEM(counts.shape, jnp.int32),
            pltpu.SemaphoreType.DMA((2,)),
        ],
        compiler_params=PARAMS,
        cost_estimate=pl.CostEstimate(flops=2 * 10**8, bytes_accessed=2 * 10**6, transcendentals=0),
    )(
        pltpu.with_memory_space_constraint(intersection.T, pltpu.HBM),
        pltpu.with_memory_space_constraint(counts, pltpu.HBM),
        phi_values,
        panel_values,
        site,
    )
    projectors = proj_panel.reshape(own, -1)
    far = move(jnp.concatenate([part, projectors], axis=0), lambda x, z, s: (x, z, s ^ 2))
    other, got[3], got[1], left, far = lax.optimization_barrier((other, got[3], got[1], left, far))
    here = jnp.concatenate([part, far, projectors], axis=0)
    after = swap(here)
    swapped = {1: swap(got[1])}
    swapped[3] = swap(got[3])
    density, rho = pl.pallas_call(
        functools.partial(sum_kernel, cells),
        out_shape=(
            jax.ShapeDtypeStruct((1, cells), F32),
            jax.ShapeDtypeStruct((atoms_own, NPROJ * NPROJ), F32),
        ),
        in_specs=[VMEM] * 10,
        out_specs=(VMEM, VMEM),
        compiler_params=PARAMS,
    )(left, columns, block, other, here, after, got[1], swapped[1], got[3], swapped[3])
    return density.reshape(cells), rho


def shards(coeffs, occupations, counts, intersection, phi_values, panel_values, proj_site, proj_panel):
    n_row, n_col, n_slab = (lax.axis_size(a) for a in ("prow", "pcol", "dz"))
    rows = coeffs.shape[0]
    fits = coeffs.size * 2 * n_row * n_col <= GATHER_LIMIT
    regular = n_row == 2 and n_col == 4 and n_slab == 4 and rows >= PW and rows % 512 == 0
    plan = gather_shards if fits and regular else exchange_shards
    return plan(coeffs, occupations, counts, intersection, phi_values, panel_values, proj_site, proj_panel)


def solution(mesh):
    return jax.shard_map(
        shards,
        mesh=mesh,
        in_specs=(
            P("prow", "pcol"),
            P("pcol"),
            P(),
            P(),
            P(("prow", "pcol", "dz"), None),
            P(("prow", "pcol", "dz"), None),
            P(("prow", "pcol"), None, None),
            P(("prow", "pcol"), None, "dz"),
        ),
        out_specs=(P(("prow", "pcol", "dz")), P(("prow", "pcol"), None)),
        check_vma=False,
    )
```

```python
import functools

import jax
import jax.numpy as jnp
from jax import lax
from jax.experimental import pallas as pl
from jax.experimental.pallas import tpu as pltpu
from jax.sharding import PartitionSpec as P

SLOTS = 16
LIVE = 13
NPROJ = 16
PW = 512
CAP = 2
GATHER_LIMIT = 2**21

F32 = jnp.float32
BF16 = jnp.bfloat16


def spread(block, axis, holder):
    block = jnp.where(lax.axis_index(axis) == holder, block, jnp.zeros_like(block))
    return lax.psum(block, axis)


def exchange_shards(
    coeffs, occupations, counts, intersection, phi_values, panel_values, proj_site, proj_panel
):
    n_row = lax.axis_size("prow")
    n_col = lax.axis_size("pcol")
    n_slab = lax.axis_size("dz")
    rows_blk = coeffs.shape[0]
    atoms_blk = rows_blk // SLOTS
    start_atom = lax.axis_index("prow") * atoms_blk
    block_counts = lax.dynamic_slice_in_dim(counts, start_atom, atoms_blk)
    slot_ids = lax.broadcasted_iota(jnp.int32, (atoms_blk, SLOTS), 1)
    live = (slot_ids < block_counts[:, None]).reshape(rows_blk, 1)
    masked = jnp.where(live, coeffs, jnp.zeros((), coeffs.dtype))
    weights = (occupations.astype(jnp.float32) * 0.5).astype(coeffs.dtype)
    panel = spread(coeffs[:PW], "prow", 0)
    panel_slots = lax.broadcasted_iota(jnp.int32, (PW // SLOTS, SLOTS), 1)
    panel_live = (panel_slots < counts[: PW // SLOTS][:, None]).reshape(PW, 1)
    panel = jnp.where(panel_live, panel, jnp.zeros((), panel.dtype))
    scaled = masked * weights[None, :]
    owned = lax.psum_scatter(
        lax.dot_general(
            scaled, panel, (((1,), (1,)), ((), ())), preferred_element_type=jnp.float32
        ),
        "pcol",
        scatter_dimension=0,
        tiled=True,
    )
    owned_rows = owned.astype(jnp.bfloat16)
    atoms_own = owned_rows.shape[0] // SLOTS
    owned_blocks = owned_rows.reshape(atoms_own, SLOTS, PW)
    owner_id = lax.axis_index("prow") * n_col + lax.axis_index("pcol")
    slab = lax.axis_index("dz")
    receivers = n_row * n_col
    by_slab = intersection.reshape(receivers, n_slab, intersection.shape[1])
    lists = lax.dynamic_index_in_dim(by_slab, slab, 1, keepdims=False)
    mine = lists // atoms_own == owner_id
    ranks = jnp.cumsum(mine.astype(jnp.int32), axis=1) - 1
    slot_pick = lax.broadcasted_iota(jnp.int32, (1, 1, CAP), 2)
    picked = mine[:, :, None] & (ranks[:, :, None] == slot_pick)
    local_atom = jnp.sum(jnp.where(picked, (lists - owner_id * atoms_own)[:, :, None], 0), axis=1)
    valid = jnp.any(picked, axis=1)
    outgoing = jnp.where(
        valid[:, :, None, None], owned_blocks[local_atom], jnp.zeros((), owned_rows.dtype)
    )
    incoming = lax.all_to_all(
        outgoing.reshape(receivers * CAP * SLOTS, PW),
        ("prow", "pcol"),
        split_axis=0,
        concat_axis=0,
        tiled=True,
    )
    incoming = incoming.reshape(receivers * CAP, SLOTS, PW)
    domain = owner_id * n_slab + slab
    wanted = lax.dynamic_index_in_dim(intersection, domain, 0, keepdims=False)
    wanted_owner = wanted // atoms_own
    listed = wanted.shape[0]
    same_owner = wanted_owner[:, None] == wanted_owner[None, :]
    earlier = lax.broadcasted_iota(jnp.int32, (listed, listed), 1) < lax.broadcasted_iota(
        jnp.int32, (listed, listed), 0
    )
    rank_in = jnp.sum((same_owner & earlier).astype(jnp.int32), axis=1)
    slot_of = wanted_owner * CAP + rank_in
    domain_rows = incoming[slot_of].reshape(listed * SLOTS, PW)
    mixed = jnp.dot(phi_values, domain_rows, preferred_element_type=jnp.float32)
    density = jnp.sum(mixed * panel_values.astype(jnp.float32), axis=1)
    projected = jnp.einsum(
        "aim,amn->ain", proj_site, owned_blocks, preferred_element_type=jnp.float32
    )
    slab_cols = proj_panel.shape[2]
    part_proj = lax.dynamic_slice_in_dim(projected, slab * slab_cols, slab_cols, 2)
    partial_rho = jnp.einsum(
        "ain,ajn->aij", part_proj, proj_panel.astype(jnp.float32), precision=lax.Precision.HIGHEST
    )
    rho_full = lax.psum(partial_rho, "dz")
    return (density, rho_full.reshape(atoms_own, NPROJ * NPROJ))


def iota(shape, dim):
    return lax.broadcasted_iota(jnp.int32, shape, dim)


def pick(condition):
    return jnp.where(condition, 1.0, 0.0).astype(BF16)


def take(left, right):
    return jnp.dot(left, right, preferred_element_type=F32).astype(BF16)


def packed_rows(rows):
    return rows // SLOTS * LIVE + 16


def pack_kernel(occ_ref, coeffs_ref, out_ref, half_ref, occ, held, arrived):
    rows = coeffs_ref.shape[0]
    group = 16
    span = group * SLOTS
    groups = rows // span
    copies = [
        pltpu.make_async_copy(coeffs_ref, held, arrived.at[0]),
        pltpu.make_async_copy(occ_ref, occ, arrived.at[1]),
    ]
    for copy in copies:
        copy.start()
    old = iota((group * LIVE, span), 1)
    slot = old & (SLOTS - 1)
    move = pick(((old >> 4) * LIVE + slot == iota((group * LIVE, span), 0)) & (slot < LIVE))
    tiles = []
    for copy in copies:
        copy.wait()
    for g in range(groups):
        tiles.append(take(move, held[g * span : (g + 1) * span, :]))
        out_ref[g * group * LIVE : (g + 1) * group * LIVE, :] = tiles[-1]
    weights = occ[...].reshape(1, occ.shape[0]).astype(F32) * 0.5
    weights = jnp.broadcast_to(weights, (16, weights.shape[1])).astype(BF16)
    out_ref[rows // SLOTS * LIVE :, :] = weights
    odd = (lax.axis_index("dz") & 1) == 1
    size = half_ref.shape[0] - 16
    for t in range(groups // 2):
        at = t * group * LIVE
        half_ref[at : at + group * LIVE, :] = jnp.where(odd, tiles[groups // 2 + t], tiles[t])
    half_ref[size:, :] = weights


def panel_map(counts_ref, packed):
    slot = iota((SLOTS, packed), 0)
    new = iota((SLOTS, packed), 1)
    return jnp.concatenate(
        [pick((new == t * LIVE + slot) & (slot < counts_ref[t])) for t in range(PW // SLOTS)], axis=0
    )


def left_kernel(
    n_col,
    n_slab,
    lists_hbm,
    counts_hbm,
    phi_ref,
    panel_ref,
    site_ref,
    out_ref,
    columns_ref,
    lists_ref,
    counts_ref,
    arrived,
):
    copies = [
        pltpu.make_async_copy(source, target, arrived.at[i])
        for i, (source, target) in enumerate(((lists_hbm, lists_ref), (counts_hbm, counts_ref)))
    ]
    for copy in copies:
        copy.start()
    for copy in copies:
        copy.wait()
    x, z, s = lax.axis_index("prow"), lax.axis_index("pcol"), lax.axis_index("dz")
    cells, listed = phi_ref.shape[0], lists_ref.shape[0]
    packed = out_ref.shape[2]
    own = site_ref.shape[0]
    atoms_own = own // NPROJ
    blk_atoms = (packed - 16) // LIVE
    domain = (x * n_col + z) * n_slab + s
    slot = iota((SLOTS, packed), 0)
    new = iota((SLOTS, packed), 1)
    spread_lanes = pick(iota((SLOTS, own), 0) == (iota((SLOTS, own), 1) & (SLOTS - 1)))
    tiled = take(site_ref[...], spread_lanes)
    mine = (iota((own, own), 0) & (atoms_own - 1)) == (iota((own, own), 1) >> 4)
    tiled = jnp.where(mine, tiled, jnp.zeros_like(tiled))
    first = z * atoms_own
    to_own = jnp.concatenate(
        [
            pick((new == (first + a) * LIVE + slot) & (slot < counts_ref[x * blk_atoms + first + a]))
            for a in range(atoms_own)
        ],
        axis=0,
    )
    site_side = take(tiled, to_own)
    for b in range(2):
        to_listed = jnp.concatenate(
            [
                pick(
                    (new == (lists_ref[p, domain] - b * blk_atoms) * LIVE + slot)
                    & (slot < counts_ref[lists_ref[p, domain]])
                    & (new < blk_atoms * LIVE)
                )
                for p in range(listed)
            ],
            axis=0,
        )
        out_ref[b, 0:cells, :] = take(phi_ref[...], to_listed)
        out_ref[b, 2 * cells : 2 * cells + own, :] = jnp.where(x == b, site_side, jnp.zeros_like(site_side))
    columns = panel_map(counts_ref, packed)
    columns_ref[...] = columns
    out_ref[0, cells : 2 * cells, :] = take(panel_ref[...], columns)
    out_ref[1, cells : 2 * cells, :] = jnp.zeros((cells, packed), BF16)


def split(values):
    high = values.astype(BF16)
    return high, (values - high.astype(F32)).astype(BF16)


def partial_sums(a, b, near, cells, left_ref, proj_ref):
    weight_row = left_ref.shape[2] - 16
    r = jnp.dot(left_ref[near], a, preferred_element_type=F32)
    r += jnp.dot(left_ref[1 - near], b, preferred_element_type=F32)
    right = jnp.dot(proj_ref[...], jnp.where(near == 0, a, b), preferred_element_type=F32)
    f = a[weight_row:, :].astype(F32)[0:1]
    term = r[:cells] * f * r[cells : 2 * cells]
    term = sum(term[:, at : at + cells] for at in range(0, term.shape[1], cells))
    high, low = split(r[2 * cells :] * f)
    right_high, right_low = split(right)
    rho = sum(
        lax.dot_general(one, two, (((1,), (1,)), ((), ())), preferred_element_type=F32)
        for one, two in ((high, right_high), (low, right_high), (high, right_low))
    )
    return term, rho


def early_kernel(
    cells, left_ref, columns_ref, a_ref, b_ref, here_ref, next_ref, term_ref, rho_ref, proj_ref
):
    x, s = lax.axis_index("prow"), lax.axis_index("dz")
    odd, back = (s & 1) == 1, (s & 2) == 2
    here, after = here_ref[...], next_ref[...]
    evens, odds = jnp.where(odd, after, here), jnp.where(odd, here, after)
    half = (left_ref.shape[2] - 16) // 2
    size = half + 16

    def joined(at):
        return jnp.concatenate([evens[at : at + half], odds[at : at + size]], axis=0)

    one, two = joined(0), joined(size)
    a = jnp.concatenate([a_ref[...], jnp.where(back, two, one)], axis=1)
    b = jnp.concatenate([b_ref[...], jnp.where(back, one, two)], axis=1)
    own = proj_ref.shape[0]
    far, near = 2 * size, 2 * size + own
    front = [jnp.where(back, part[far:near], part[near:]) for part in (evens, odds)]
    rear = [jnp.where(back, part[near:], part[far:near]) for part in (evens, odds)]
    proj_ref[...] = take(jnp.concatenate(front + rear, axis=1), columns_ref[...])
    term_ref[...], rho_ref[...] = partial_sums(a, b, x, cells, left_ref, proj_ref)


def late_kernel(cells, left_ref, proj_ref, a_ref, b_ref, c_ref, d_ref, term_ref, part_ref, density_ref, rho_ref):
    near = lax.axis_index("prow") ^ (lax.axis_index("dz") & 1)
    a = jnp.concatenate([a_ref[...], c_ref[...]], axis=1)
    b = jnp.concatenate([b_ref[...], d_ref[...]], axis=1)
    term, rho = partial_sums(a, b, near, cells, left_ref, proj_ref)
    term += term_ref[...]
    rho += part_ref[...]
    density_ref[...] = jnp.sum(term.T, axis=0, keepdims=True)
    own = proj_ref.shape[0]
    atoms = own // NPROJ
    rho = jnp.where((iota((own, own), 0) & (atoms - 1)) == (iota((own, own), 1) >> 4), rho, 0.0)
    wide = NPROJ * NPROJ
    fold = pick((iota((own, wide), 0) & (NPROJ - 1)) == (iota((own, wide), 1) & (NPROJ - 1)))
    rows = sum(jnp.dot(part, fold, preferred_element_type=F32) for part in split(rho))
    keep = (iota((own, wide), 0) // atoms) == (iota((own, wide), 1) >> 4)
    rho_ref[...] = jnp.sum(jnp.where(keep, rows, 0.0).reshape(NPROJ, atoms, wide), axis=0)


VMEM = pl.BlockSpec(memory_space=pltpu.VMEM)
SMEM = pl.BlockSpec(memory_space=pltpu.SMEM)
HBM = pl.BlockSpec(memory_space=pltpu.HBM)
PARAMS = pltpu.CompilerParams(vmem_limit_bytes=32 * 2**20)


def gather_shards(
    coeffs, occupations, counts, intersection, phi_values, panel_values, proj_site, proj_panel
):
    n_row, n_col, n_slab = (lax.axis_size(a) for a in ("prow", "pcol", "dz"))
    axes = ("prow", "pcol", "dz")

    def move(block, target):
        pairs = []
        for i in range(n_row * n_col * n_slab):
            x, z, s = i // (n_col * n_slab), i // n_slab % n_col, i % n_slab
            tx, tz, ts = target(x, z, s)
            pairs.append((i, (tx * n_col + tz) * n_slab + ts))
        return lax.ppermute(block, axes, pairs)

    def swap(block):
        return move(block, lambda x, z, s: (x, z, s ^ 1))

    rows, states = coeffs.shape
    packed = packed_rows(rows)
    atoms_own = proj_site.shape[0]
    own = atoms_own * NPROJ
    cells = phi_values.shape[0]
    half = packed_rows(rows // 2)
    block, part = pl.pallas_call(
        pack_kernel,
        out_shape=(
            jax.ShapeDtypeStruct((packed, states), BF16),
            jax.ShapeDtypeStruct((half, states), BF16),
        ),
        in_specs=[HBM, HBM],
        out_specs=(VMEM, VMEM),
        scratch_shapes=[
            pltpu.VMEM((states,), jnp.int32),
            pltpu.VMEM((rows, states), BF16),
            pltpu.SemaphoreType.DMA((2,)),
        ],
        compiler_params=PARAMS,
    )(
        pltpu.with_memory_space_constraint(occupations, pltpu.HBM),
        pltpu.with_memory_space_constraint(coeffs, pltpu.HBM),
    )
    part = move(part, lambda x, z, s: (x ^ (s >> 1 & 1), z ^ 2, s))
    got = {k: move(block, lambda x, z, s: (x ^ (s & 1), z ^ k, s)) for k in (1, 3)}
    other = move(block, lambda x, z, s: (x ^ 1, z, s))
    site = proj_site.transpose(1, 0, 2).reshape(own, SLOTS)
    left, columns = pl.pallas_call(
        functools.partial(left_kernel, n_col, n_slab),
        out_shape=(
            jax.ShapeDtypeStruct((2, 2 * cells + own, packed), BF16),
            jax.ShapeDtypeStruct((PW, packed), BF16),
        ),
        in_specs=[HBM, HBM, VMEM, VMEM, VMEM],
        out_specs=(VMEM, VMEM),
        scratch_shapes=[
            pltpu.SMEM(intersection.shape[::-1], jnp.int32),
            pltpu.SMEM(counts.shape, jnp.int32),
            pltpu.SemaphoreType.DMA((2,)),
        ],
        compiler_params=PARAMS,
        cost_estimate=pl.CostEstimate(flops=2 * 10**8, bytes_accessed=2 * 10**6, transcendentals=0),
    )(
        pltpu.with_memory_space_constraint(intersection.T, pltpu.HBM),
        pltpu.with_memory_space_constraint(counts, pltpu.HBM),
        phi_values,
        panel_values,
        site,
    )
    projectors = proj_panel.reshape(own, -1)
    far = move(jnp.concatenate([part, projectors], axis=0), lambda x, z, s: (x, z, s ^ 2))
    got[1], got[3], other, left, far = lax.optimization_barrier((got[1], got[3], other, left, far))
    here = jnp.concatenate([part, far, projectors], axis=0)
    after = swap(here)
    swapped = {1: swap(got[1])}
    term, rho, proj = pl.pallas_call(
        functools.partial(early_kernel, cells),
        out_shape=(
            jax.ShapeDtypeStruct((cells, states), F32),
            jax.ShapeDtypeStruct((own, own), F32),
            jax.ShapeDtypeStruct((own, packed), BF16),
        ),
        in_specs=[VMEM] * 6,
        out_specs=(VMEM, VMEM, VMEM),
        compiler_params=PARAMS,
    )(left, columns, block, other, here, after)
    swapped[3] = swap(got[3])
    density, rho = pl.pallas_call(
        functools.partial(late_kernel, cells),
        out_shape=(
            jax.ShapeDtypeStruct((1, cells), F32),
            jax.ShapeDtypeStruct((atoms_own, NPROJ * NPROJ), F32),
        ),
        in_specs=[VMEM] * 8,
        out_specs=(VMEM, VMEM),
        compiler_params=PARAMS,
    )(left, proj, got[1], swapped[1], got[3], swapped[3], term, rho)
    return density.reshape(cells), rho


def shards(coeffs, occupations, counts, intersection, phi_values, panel_values, proj_site, proj_panel):
    n_row, n_col, n_slab = (lax.axis_size(a) for a in ("prow", "pcol", "dz"))
    rows = coeffs.shape[0]
    fits = coeffs.size * 2 * n_row * n_col <= GATHER_LIMIT
    regular = n_row == 2 and n_col == 4 and n_slab == 4 and rows >= PW and rows % 256 == 0
    plan = gather_shards if fits and regular else exchange_shards
    return plan(coeffs, occupations, counts, intersection, phi_values, panel_values, proj_site, proj_panel)


def solution(mesh):
    return jax.shard_map(
        shards,
        mesh=mesh,
        in_specs=(
            P("prow", "pcol"),
            P("pcol"),
            P(),
            P(),
            P(("prow", "pcol", "dz"), None),
            P(("prow", "pcol", "dz"), None),
            P(("prow", "pcol"), None, None),
            P(("prow", "pcol"), None, "dz"),
        ),
        out_specs=(P(("prow", "pcol", "dz")), P(("prow", "pcol"), None)),
        check_vma=False,
    )
```
